32 devices in a mesh: ctx: 4 (over z), fsdp: 8 (over y, x, core).
Axes of the slice: x: 2, y: 2, z: 4, core: 2. Of those that a mesh axis runs over, the one named last changes fastest.
Arguments:
- activations: bfloat16 [8, 2, 1024, 2560], P('fsdp', None, 'ctx'), may hold values from -6 to 6
- cotangent: bfloat16 [8, 2, 1024, 2560], P('fsdp', None, 'ctx'), may hold values from -6 to 6
- seq_length: int32 [8, 2], P('fsdp'), may hold values from 513 to 1024
- block_order: int32 [8], replicated, may hold values from 0 to 7, each once
- attn_norm: bfloat16 [2560], P('fsdp'), may hold values from 0.5 to 1.5
- query_down: bfloat16 [2560, 768], P('fsdp'), may hold values from -0.125 to 0.125
- query_norm: bfloat16 [768], P('fsdp'), may hold values from 0.5 to 1.5
- query_up: bfloat16 [768, 3840], P('fsdp'), may hold values from -0.21875 to 0.21875
- latent_down: bfloat16 [2560, 288], P('fsdp'), may hold values from -0.125 to 0.125
- latent_norm: bfloat16 [256], P('fsdp'), may hold values from 0.5 to 1.5
- latent_up: bfloat16 [256, 5120], P('fsdp'), may hold values from -0.375 to 0.375
- attn_out: bfloat16 [2560, 2560], P('fsdp'), may hold values from -4 to 4
- mlp_norm: bfloat16 [2560], P('fsdp'), may hold values from 0.5 to 1.5
- gate_weight: bfloat16 [6400, 2560], P('fsdp'), may hold values from -0.125 to 0.125
- up_weight: bfloat16 [6400, 2560], P('fsdp'), may hold values from -0.125 to 0.125
- down_weight: bfloat16 [6400, 2560], P('fsdp'), may hold values from -0.875 to 0.875
Outputs:
- output: bfloat16 [8, 2, 1024, 2560], P('fsdp', None, 'ctx')
- input_grad: bfloat16 [8, 2, 1024, 2560], P('fsdp', None, 'ctx')
- attn_norm_grad: float32 [2560], P('fsdp')
- query_down_grad: float32 [2560, 768], P('fsdp')
- query_norm_grad: float32 [768], P('fsdp')
- query_up_grad: float32 [768, 3840], P('fsdp')
- latent_down_grad: float32 [2560, 288], P('fsdp')
- latent_norm_grad: float32 [256], P('fsdp')
- latent_up_grad: float32 [256, 5120], P('fsdp')
- attn_out_grad: float32 [2560, 2560], P('fsdp')
- mlp_norm_grad: float32 [2560], P('fsdp')
- gate_weight_grad: float32 [6400, 2560], P('fsdp')
- up_weight_grad: float32 [6400, 2560], P('fsdp')
- down_weight_grad: float32 [6400, 2560], P('fsdp')
The draws below stay inside these ranges and needn't reach their ends.
All inputs are finite; a program needn't handle non-finite values.
Results may differ from the reference program's by a relative error of at most 0.024.
Values may be sent and summed in bfloat16 or wider, within the bound.
No kernel may reach another device: no remote copies, remote signals or barrier semaphores. Data moves between devices by JAX's collectives and lax.ppermute only.
A program may use at most 576 MiB of HBM per device.

```python
import math
import jax
import jax.numpy as jnp
from jax import lax

D = 2560
H = 40
DN = 64
DR = 32
DV = 64
QR = 768
KVR = 256
FF = 6400
SEQ = 1024
MB = 2
GROUPS = 8
N_CTX = 4


def touch_ends(values, key, low, largest):
    longest = values.shape.index(max(values.shape))
    spots = []
    for shift in (0, 1):
        where = [jax.random.randint(jax.random.fold_in(key, axis), (), 0, length) for axis, length in enumerate(values.shape)]
        where[longest] = (where[longest] + shift) % values.shape[longest]
        spots.append(tuple(where))
    return values.at[spots[0]].set(low).at[spots[1]].set(largest)


def level_of(key, dims, pieces, low, top_value):
    def one(dim, parts):
        steps = jax.random.uniform(jax.random.fold_in(jax.random.fold_in(key, 6), dim), (parts,), jnp.float32, low / len(pieces), top_value / len(pieces))
        return jnp.repeat(jnp.exp(steps), dims[dim] // parts).reshape((-1,) + (1,) * (len(dims) - dim - 1))

    level = one(*pieces[0])
    for cut in pieces[1:]:
        level = level * one(*cut)
    return level


def normal_values(key, shape, scale, bound, shards=(), held_as=jnp.bfloat16):
    factor_of = level_of(key, shape, shards, -0.22, 0.18) if shards else 1.0
    values = jax.random.normal(key, shape, jnp.float32) * scale * factor_of
    return jnp.minimum(jnp.maximum(values, -bound), bound).astype(held_as)


def setup_inputs(seed: int = 0) -> dict:
    splits = jax.random.split(jax.random.key(seed), 17)
    activations = normal_values(splits[0], (GROUPS, MB, SEQ, D), 1.0, 6.0, ((0, 8), (2, 4)))
    cotangent = normal_values(splits[1], (GROUPS, MB, SEQ, D), 1.0, 6.0, ((0, 8), (2, 4)))
    seq_length = touch_ends(jax.random.randint(splits[2], (GROUPS, MB), SEQ // 2 + 1, SEQ + 1), jax.random.fold_in(splits[2], 1), SEQ // 2 + 1, SEQ).astype(jnp.int32)
    block_order = jax.random.permutation(splits[3], 2 * N_CTX).astype(jnp.int32)
    attn_norm = jnp.clip(1.0 + 0.1 * jax.random.normal(splits[4], (D,), jnp.float32), 0.5, 1.5).astype(jnp.bfloat16)
    query_down = normal_values(splits[5], (D, QR), D ** -0.5, 0.125, ((0, 8),))
    query_norm = jnp.clip(1.0 + 0.1 * jax.random.normal(splits[6], (QR,), jnp.float32), 0.5, 1.5).astype(jnp.bfloat16)
    query_up = normal_values(splits[7], (QR, H * (DN + DR)), QR ** -0.5, 0.21875, ((0, 8),))
    latent_down = normal_values(splits[8], (D, KVR + DR), D ** -0.5, 0.125, ((0, 8),))
    latent_norm = jnp.clip(1.0 + 0.1 * jax.random.normal(splits[9], (KVR,), jnp.float32), 0.5, 1.5).astype(jnp.bfloat16)
    latent_up = normal_values(splits[10], (KVR, H * (DN + DV)), KVR ** -0.5, 0.375, ((0, 8),))
    attn_out = normal_values(splits[11], (H * DV, D), 0.7, 4.0, ((0, 8),))
    mlp_norm = jnp.clip(1.0 + 0.1 * jax.random.normal(splits[12], (D,), jnp.float32), 0.5, 1.5).astype(jnp.bfloat16)
    gate_weight = normal_values(splits[13], (FF, D), D ** -0.5, 0.125, ((0, 8),))
    up_weight = normal_values(splits[14], (FF, D), D ** -0.5, 0.125, ((0, 8),))
    down_weight = normal_values(splits[15], (FF, D), (max(FF // 128, 1)) ** -0.5, 0.875, ((0, 8),))
    return dict(activations=activations, cotangent=cotangent, seq_length=seq_length, block_order=block_order, attn_norm=attn_norm, query_down=query_down, query_norm=query_norm, query_up=query_up, latent_down=latent_down, latent_norm=latent_norm, latent_up=latent_up, attn_out=attn_out, mlp_norm=mlp_norm, gate_weight=gate_weight, up_weight=up_weight, down_weight=down_weight)


@jax.custom_vjp
def low(v):
    return lax.optimization_barrier(v.astype(jnp.bfloat16)).astype(jnp.float32)

@jax.custom_vjp
def low_back(v):
    return v

def low_keep(v):
    return (low(v), None)

def low_pass(kept, grad):
    return (grad,)

def back_keep(v):
    return (v, None)

def back_low(kept, grad):
    return (low(grad),)
low.defvjp(low_keep, low_pass)
low_back.defvjp(back_keep, back_low)
branch_scale = 1.4 / math.sqrt(62.0)
norm_eps = 1e-05
rope_base = 10000.0
highest = lax.Precision.HIGHEST
lowest_score = -1e+30

def rms_scale(values, gain):
    return values * lax.rsqrt(lax.optimization_barrier(jnp.mean(values * values, axis=-1, keepdims=True)) + norm_eps) * gain

def rope_tables(positions, width):
    half = width // 2
    freq = rope_base ** (-(jnp.arange(half, dtype=jnp.float32) * 2.0 / width))
    angle = positions.astype(jnp.float32)[:, None] * freq[None, :]
    return (jnp.concatenate([jnp.cos(angle), jnp.cos(angle)], axis=-1), jnp.concatenate([jnp.sin(angle), jnp.sin(angle)], axis=-1))

def turn_half(values):
    half = values.shape[-1] // 2
    return jnp.concatenate([-values[..., half:], values[..., :half]], axis=-1)

def rope_apply(values, cosine, sine):
    return values * cosine + turn_half(values) * sine

def matmul(left, right):
    return jnp.dot(left, right, precision=highest)

def layer_one(inputs, positions, length, weights):
    attn_norm, query_down, query_norm, query_up, latent_down, latent_norm, latent_up, attn_out, mlp_norm, gate_weight, up_weight, down_weight = weights
    count = inputs.shape[0]
    cosine, sine = rope_tables(positions, DR)
    first = low(rms_scale(inputs, attn_norm))
    query_latent = low_back(matmul(first, query_down))
    query_normed = low(rms_scale(query_latent, query_norm))
    query_raw = low_back(matmul(query_normed, query_up)).reshape(count, H, DN + DR)
    query = low(jnp.concatenate([query_raw[..., :DN], rope_apply(query_raw[..., DN:], cosine[:, None, :], sine[:, None, :])], axis=-1))
    latent_raw = low_back(matmul(first, latent_down))
    latent = low(rms_scale(latent_raw[:, :KVR], latent_norm))
    key_rope = low(rope_apply(latent_raw[:, KVR:], cosine, sine))
    expanded = low(matmul(latent, latent_up)).reshape(count, H, DN + DV)
    key_nope = expanded[..., :DN]
    value_rows = expanded[..., DN:]
    score_scale = (DN + DR) ** (-0.5)
    scores = (jnp.einsum('ihd,jhd->hij', query[..., :DN], key_nope, precision=highest) + jnp.einsum('ihd,jd->hij', query[..., DN:], key_rope, precision=highest)) * score_scale
    scores = low_back(scores)
    allowed = (positions[None, :] <= positions[:, None]) & (positions[None, :] < length)
    masked = jnp.where(allowed[None], scores, lowest_score)
    row_top = lax.optimization_barrier(jnp.max(masked, axis=-1, keepdims=True))
    expo = jnp.exp(masked - row_top)
    probs = low(expo / lax.optimization_barrier(jnp.sum(expo, axis=-1, keepdims=True)))
    mixed = jnp.einsum('hij,jhd->ihd', probs, value_rows, precision=highest).reshape(count, H * DV)
    mixed = low_back(low(mixed))
    attn_branch = low_back(matmul(mixed, attn_out))
    resid = inputs + branch_scale * attn_branch
    second = low(rms_scale(resid, mlp_norm))
    gate = low_back(jnp.dot(second, gate_weight.T, precision=highest))
    upval = low_back(jnp.dot(second, up_weight.T, precision=highest))
    hidden = low(jax.nn.silu(gate) * upval)
    ffn = low_back(matmul(hidden, down_weight))
    return resid + branch_scale * ffn

def reference(activations, cotangent, seq_length, block_order, attn_norm, query_down, query_norm, query_up, latent_down, latent_norm, latent_up, attn_out, mlp_norm, gate_weight, up_weight, down_weight):
    seq_rows = activations.shape[2]
    block_size = seq_rows // block_order.shape[0]
    every_row = jnp.arange(seq_rows, dtype=jnp.int32)
    positions = (block_order[every_row // block_size] * block_size + every_row % block_size).astype(jnp.int32)
    flat_inputs = activations.reshape(-1, seq_rows, D).astype(jnp.float32)
    flat_length = seq_length.reshape(-1).astype(jnp.int32)
    live = (positions[None, :] < flat_length[:, None]).astype(jnp.float32)
    flat_cot = cotangent.reshape(-1, seq_rows, D).astype(jnp.float32) * live[..., None]
    weights = (attn_norm.astype(jnp.float32), query_down.astype(jnp.float32), query_norm.astype(jnp.float32), query_up.astype(jnp.float32), latent_down.astype(jnp.float32), latent_norm.astype(jnp.float32), latent_up.astype(jnp.float32), attn_out.astype(jnp.float32), mlp_norm.astype(jnp.float32), gate_weight.astype(jnp.float32), up_weight.astype(jnp.float32), down_weight.astype(jnp.float32))
    layer_saved = jax.checkpoint(layer_one)

    def forward(inputs_all, weight_tuple):

        def step(carry, item):
            return (carry, layer_saved(item[0], positions, item[1], weight_tuple))
        unused, result = lax.scan(step, None, (inputs_all, flat_length))
        return result
    result, pullback = jax.vjp(forward, flat_inputs, weights)
    input_grad, grads = pullback(flat_cot)
    return (result.reshape(activations.shape).astype(jnp.bfloat16), input_grad.reshape(activations.shape).astype(jnp.bfloat16), grads[0], grads[1], grads[2], grads[3], grads[4], grads[5], grads[6], grads[7], grads[8], grads[9], grads[10], grads[11])
```

```python
import functools
import math

import jax
import jax.numpy as jnp
from jax import lax
from jax.experimental import pallas as pl
from jax.experimental.pallas import tpu as pltpu
from jax.sharding import PartitionSpec as P

H = 40
DN = 64
DR = 32
DV = 64
KVR = 256
QUAD = 4


branch_scale = 1.4 / math.sqrt(62.0)
norm_eps = 1e-05
rope_base = 10000.0
lowest_score = -1e30
score_scale = (DN + DR) ** -0.5
exp_scale = math.log2(math.e) * score_scale


def rms_scale(values, gain):
    inverse = lax.rsqrt(jnp.mean(values * values, axis=-1, keepdims=True) + norm_eps)
    plain = values * inverse
    return (plain * gain, plain, inverse)


def rms_back(grad_out, plain, inverse, gain):
    gain_grad = jnp.sum(grad_out * plain, axis=0)
    scaled = grad_out * gain
    values_grad = inverse * (scaled - plain * jnp.mean(scaled * plain, axis=-1, keepdims=True))
    return (values_grad, gain_grad)


def rope_tables(positions, width):
    half = width // 2
    freq = rope_base ** (-(jnp.arange(half, dtype=jnp.float32) * 2.0 / width))
    angle = positions.astype(jnp.float32)[:, None] * freq[None, :]
    return (
        jnp.concatenate([jnp.cos(angle), jnp.cos(angle)], axis=-1),
        jnp.concatenate([jnp.sin(angle), jnp.sin(angle)], axis=-1),
    )


def turn_half(values):
    half = values.shape[-1] // 2
    return jnp.concatenate([-values[..., half:], values[..., :half]], axis=-1)


def turn_back(values):
    half = values.shape[-1] // 2
    return jnp.concatenate([values[..., half:], -values[..., :half]], axis=-1)


def rope_apply(values, cosine, sine):
    return values * cosine + turn_half(values) * sine


def rope_back(grads, cosine, sine):
    return grads * cosine + turn_back(grads * sine)


def matmul_plain(left, right):
    return jnp.dot(left, right, preferred_element_type=jnp.float32)


def matmul_left(left, right):
    return lax.dot_general(
        left, right, (((0,), (0,)), ((), ())), preferred_element_type=jnp.float32
    )


def matmul_right(left, right):
    return lax.dot_general(
        left, right, (((1,), (1,)), ((), ())), preferred_element_type=jnp.float32
    )


def flip(values, bit):
    count = lax.axis_size("fsdp")
    return lax.ppermute(values, "fsdp", [(i, i ^ bit) for i in range(count)])


def chip_bits():
    return [1 << k for k in range(1, lax.axis_size("fsdp").bit_length() - 1)]


def low(values):
    return values.astype(jnp.bfloat16)


def add_up(left, right):
    return left.astype(jnp.float32) + right.astype(jnp.float32)


def place_kernel(plan, me_ref, *refs):
    sources, outs, sems = refs[: len(plan)], refs[len(plan) : -1], refs[-1]
    me = me_ref[0]
    copies = []
    for source, (out, rows, places, stride, offset) in zip(sources, plan):
        for k, place in enumerate(places):
            start = pl.multiple_of((me ^ place) * stride + offset, 16)
            copies.append(
                pltpu.make_async_copy(
                    source.at[pl.ds(k * rows, rows)],
                    outs[out].at[pl.ds(start, rows)],
                    sems.at[len(copies)],
                )
            )
    for copy in copies:
        copy.start()
    for copy in copies:
        copy.wait()


def place_shards(groups):
    count = lax.axis_size("fsdp")
    me = lax.axis_index("fsdp").astype(jnp.int32).reshape(1)
    plan, sources, shapes = [], [], []
    for out, parts in enumerate(groups):
        heights = [held.shape[0] * 2 // count for held, _, _ in parts]
        offset = 0
        for (held, other, order), rows in zip(parts, heights):
            places = [0]
            for bit in order:
                places = places + [place ^ bit for place in places]
            plan.append((out, rows, tuple(places), sum(heights), offset))
            plan.append((out, rows, tuple(place ^ 1 for place in places), sum(heights), offset))
            sources += [held, other]
            offset += rows
        shapes.append(jax.ShapeDtypeStruct((count * sum(heights), parts[0][0].shape[1]), jnp.bfloat16))
    anywhere = pl.BlockSpec(memory_space=pl.ANY)
    return pl.pallas_call(
        functools.partial(place_kernel, tuple(plan)),
        in_specs=[pl.BlockSpec(memory_space=pltpu.SMEM)] + [anywhere] * len(sources),
        out_specs=[pl.BlockSpec(memory_space=pltpu.VMEM)] * len(shapes),
        out_shape=shapes,
        scratch_shapes=[pltpu.SemaphoreType.DMA((len(plan) * count // 2,))],
        compiler_params=pltpu.CompilerParams(vmem_limit_bytes=32 * 2**20),
        name="place_shards",
    )(me, *sources)


class ScatterWhole:
    def __init__(self, held, order):
        self.held = held
        self.order = list(order)
        self.left = [1 << k for k in range(held.shape[0].bit_length() - 2, -1, -1)]
        self.me = lax.axis_index("fsdp")

    def send(self):
        rows, width = self.held.shape[1:]
        place = self.left.index(self.order[0])
        below = 1 << (len(self.left) - place - 1)
        held = self.held.reshape(-1, 2, below, rows, width)
        mine = (self.me // self.order[0]) % 2
        self.kept = lax.dynamic_index_in_dim(held, mine, 1, keepdims=False)
        return lax.dynamic_index_in_dim(held, 1 - mine, 1, keepdims=False)

    def move(self, value):
        return flip(value, self.order[0])

    def absorb(self, value):
        self.held = low(add_up(self.kept, value)).reshape((-1,) + self.held.shape[1:])
        self.left.remove(self.order.pop(0))


def lane_part(values, width, place):
    lane = lax.broadcasted_iota(jnp.int32, values.shape, 1)
    return jnp.where(lane // width == place, values, 0.0)


def pair_rows(nope, rope, pair):
    both = nope[:, pair * 2 * DN : (pair + 1) * 2 * DN]
    return low(
        jnp.concatenate(
            [
                jnp.concatenate(
                    [lane_part(both, DN, head), lane_part(rope, DR, 2 * pair + head)], axis=1
                )
                for head in range(2)
            ],
            axis=0,
        )
    )


def forward_kernel(
    low_ref, latent_ref, rope_ref, bias_ref, cos_ref, ahead_ref, behind_ref,
    query_w, key_w, value_w, query_ref, mixed_ref, total_ref,
):
    rows = low_ref.shape[1]
    raw = matmul_plain(low_ref[0], query_w[...])
    nope = raw[:, : QUAD * DN]
    rope = raw[:, QUAD * DN :]
    lanes = QUAD * DR
    rope = (
        rope * cos_ref[...]
        + pltpu.roll(rope, lanes - DR // 2, 1) * ahead_ref[...]
        + pltpu.roll(rope, DR // 2, 1) * behind_ref[...]
    )
    query_ref[0] = low(jnp.concatenate([nope, rope], axis=1))
    latent = latent_ref[0]
    keys = low(matmul_plain(latent, key_w[...]))
    values = low(matmul_plain(latent, value_w[...])).T
    mixed = []
    for pair in range(2):
        key_cat = jnp.concatenate(
            [keys[:, pair * 2 * DN : (pair + 1) * 2 * DN], rope_ref[0]], axis=1
        )
        scores = matmul_right(key_cat, pair_rows(nope, rope, pair))
        for head in range(2):
            place = 2 * pair + head
            own = scores[:, head * rows : (head + 1) * rows] * exp_scale + bias_ref[0]
            top = jnp.max(own, axis=0, keepdims=True)
            expo = jnp.exp2(own - top)
            total = jnp.sum(expo, axis=0, keepdims=True)
            out = matmul_plain(values[place * DV : (place + 1) * DV], low(expo))
            mixed.append(out / total)
            total_ref[0, 0, place : place + 1, :] = top + jnp.log2(total)
    mixed_ref[0] = low(jnp.concatenate(mixed, axis=0).T)


def attend_forward(query_low, latent, rope_keys, bias, cosine, ahead, behind, query_w, key_w, value_w, quads):
    batches, rows, rank = query_low.shape
    keys, width = latent.shape[1:]
    qw, kw, rw = QUAD * (DN + DR), QUAD * DN, QUAD * DR
    fixed = lambda b, j: (0, 0)
    whole = lambda b, j: (b, 0, 0)
    flops = batches * quads * (2 * keys * width * 2 * kw + 2 * rows * rank * qw + 4 * 4 * keys * rows * 256)
    return pl.pallas_call(
        forward_kernel,
        grid=(batches, quads),
        in_specs=[
            pl.BlockSpec((1, rows, rank), whole),
            pl.BlockSpec((1, keys, width), whole),
            pl.BlockSpec((1, keys, rw), whole),
            pl.BlockSpec((1, keys, rows), whole),
            pl.BlockSpec((rows, rw), fixed),
            pl.BlockSpec((rows, rw), fixed),
            pl.BlockSpec((rows, rw), fixed),
            pl.BlockSpec((rank, qw), lambda b, j: (0, j)),
            pl.BlockSpec((width, kw), lambda b, j: (0, j)),
            pl.BlockSpec((width, kw), lambda b, j: (0, j)),
        ],
        out_specs=[
            pl.BlockSpec((1, rows, qw), lambda b, j: (b, 0, j)),
            pl.BlockSpec((1, rows, kw), lambda b, j: (b, 0, j)),
            pl.BlockSpec((1, 1, QUAD, rows), lambda b, j: (b, j, 0, 0)),
        ],
        out_shape=[
            jax.ShapeDtypeStruct((batches, rows, quads * qw), jnp.bfloat16),
            jax.ShapeDtypeStruct((batches, rows, quads * kw), jnp.bfloat16),
            jax.ShapeDtypeStruct((batches, quads, QUAD, rows), jnp.float32),
        ],
        compiler_params=pltpu.CompilerParams(
            dimension_semantics=("arbitrary", "arbitrary"), vmem_limit_bytes=48 * 2**20
        ),
        cost_estimate=pl.CostEstimate(
            flops=int(flops), bytes_accessed=40 * 2**20, transcendentals=batches * quads * 4 * keys * rows
        ),
        name="attend_forward",
    )(query_low, latent, rope_keys, bias, cosine, ahead, behind, query_w, key_w, value_w)


def backward_kernel(
    query_ref, grad_ref, latent_ref, flat_ref, rope_ref, turned_ref, bias_ref, total_ref,
    cos_ref, sin_ref, key_w, value_w,
    query_out, key_up_out, value_up_out, latent_out, rope_out,
):
    rows = query_ref.shape[0]
    half = DR // 2

    @pl.when(pl.program_id(0) == 0)
    def _():
        latent_out[...] = jnp.zeros_like(latent_out)
        rope_out[...] = jnp.zeros_like(rope_out)

    latent = latent_ref[...]
    keys = low(matmul_plain(latent, key_w[...]))
    values = low(matmul_plain(latent, value_w[...]))
    turned_keys = keys.T
    query = query_ref[...].astype(jnp.float32)
    nope = query[:, : QUAD * DN]
    rope = query[:, QUAD * DN :]
    grad = grad_ref[...].astype(jnp.float32)
    key_grads, value_grads, nope_grads, rope_grads = [], [], [], []
    for pair in range(2):
        lanes = slice(pair * 2 * DN, (pair + 1) * 2 * DN)
        key_cat = jnp.concatenate([keys[:, lanes], rope_ref[...]], axis=1)
        query_cat = pair_rows(nope, rope, pair)
        grad_cat = low(
            jnp.concatenate([lane_part(grad[:, lanes], DV, head) for head in range(2)], axis=0)
        )
        scores = matmul_right(key_cat, query_cat)
        prob_grads = matmul_right(values[:, lanes], grad_cat)
        probs_low, score_low = [], []
        for head in range(2):
            place = 2 * pair + head
            cut = slice(head * rows, (head + 1) * rows)
            probs = jnp.exp2(
                scores[:, cut] * exp_scale + bias_ref[...] - total_ref[0, place : place + 1, :]
            )
            mixed = probs * prob_grads[:, cut]
            dots = jnp.sum(mixed, axis=0, keepdims=True)
            score_grad = low(mixed - probs * dots)
            probs_low.append(low(probs))
            score_low.append(score_grad)
            left = jnp.concatenate(
                [turned_keys[place * DN : (place + 1) * DN], turned_ref[...]], axis=0
            )
            turned = matmul_plain(left, score_grad) * score_scale
            nope_grads.append(turned[:DN])
            upper, lower = turned[DN : DN + half], turned[DN + half :]
            rope_grads.append(upper * cos_ref[...] + lower * sin_ref[...])
            rope_grads.append(lower * cos_ref[...] - upper * sin_ref[...])
        value_grads.append(matmul_plain(jnp.concatenate(probs_low, axis=1), grad_cat))
        key_cat_grad = matmul_plain(jnp.concatenate(score_low, axis=1), query_cat)
        key_grads.append(key_cat_grad[:, : 2 * DN])
        rope_out[...] += key_cat_grad[:, 2 * DN :] * score_scale
    query_out[...] = low(jnp.concatenate(nope_grads + rope_grads, axis=0).T)
    key_grad = low(jnp.concatenate(key_grads, axis=1) * score_scale)
    value_grad = low(jnp.concatenate(value_grads, axis=1))
    key_up_out[...] = matmul_plain(flat_ref[...], key_grad)
    value_up_out[...] = matmul_plain(flat_ref[...], value_grad)
    latent_out[...] += matmul_right(key_grad, key_w[...]) + matmul_right(value_grad, value_w[...])


def attend_backward(query, grad, latent, latent_flat, rope_keys, rope_flat, bias, totals, cos_flat, sin_flat, key_w, value_w, quads):
    rows = query.shape[0]
    keys, width = latent.shape
    qw, kw, rw = QUAD * (DN + DR), QUAD * DN, QUAD * DR
    fixed = lambda j: (0, 0)
    step = lambda j: (0, j)
    flops = quads * (2 * keys * width * 6 * kw + 5 * 4 * 2 * keys * rows * 256)
    return pl.pallas_call(
        backward_kernel,
        grid=(quads,),
        in_specs=[
            pl.BlockSpec((rows, qw), step),
            pl.BlockSpec((rows, kw), step),
            pl.BlockSpec((keys, width), fixed),
            pl.BlockSpec((width, keys), fixed),
            pl.BlockSpec((keys, rw), fixed),
            pl.BlockSpec((DR, keys), fixed),
            pl.BlockSpec((keys, rows), fixed),
            pl.BlockSpec((1, QUAD, rows), lambda j: (j, 0, 0)),
            pl.BlockSpec((DR // 2, rows), fixed),
            pl.BlockSpec((DR // 2, rows), fixed),
            pl.BlockSpec((width, kw), step),
            pl.BlockSpec((width, kw), step),
        ],
        out_specs=[
            pl.BlockSpec((rows, qw), step),
            pl.BlockSpec((width, kw), step),
            pl.BlockSpec((width, kw), step),
            pl.BlockSpec((keys, width), fixed),
            pl.BlockSpec((keys, rw), fixed),
        ],
        out_shape=[
            jax.ShapeDtypeStruct((rows, quads * qw), jnp.bfloat16),
            jax.ShapeDtypeStruct((width, quads * kw), jnp.float32),
            jax.ShapeDtypeStruct((width, quads * kw), jnp.float32),
            jax.ShapeDtypeStruct((keys, width), jnp.float32),
            jax.ShapeDtypeStruct((keys, rw), jnp.float32),
        ],
        compiler_params=pltpu.CompilerParams(
            dimension_semantics=("arbitrary",), vmem_limit_bytes=48 * 2**20
        ),
        cost_estimate=pl.CostEstimate(
            flops=int(flops), bytes_accessed=25 * 2**20, transcendentals=quads * 4 * keys * rows
        ),
        name="attend_backward",
    )(query, grad, latent, latent_flat, rope_keys, rope_flat, bias, totals, cos_flat, sin_flat, key_w, value_w)


class LineSum:
    def __init__(self):
        self.count = lax.axis_size("ctx")
        self.me = lax.axis_index("ctx")
        self.hops = self.count // 2 - 1
        self.held = []
        self.stage = []
        self.queue = []

    def add(self, *pieces):
        for piece in pieces:
            self.queue.append(len(self.held))
            self.held.append(piece)
            self.stage.append(None)

    def busy(self):
        return bool(self.queue) or any(s is not None and s >= 0 for s in self.stage)

    def outer(self, hop):
        return (self.me == hop) | (self.me == self.count - 1 - hop)

    def sends(self):
        if self.queue:
            self.stage[self.queue.pop(0)] = 0
        self.plan, values = [], []
        at = {stage: item for item, stage in enumerate(self.stage) if stage is not None}
        last = self.count - 1
        for hop in range(self.hops):
            entering, leaving = at.get(hop), at.get(2 * self.hops - hop)
            inward = [(hop, hop + 1), (last - hop, last - hop - 1)]
            outward = [(to, source) for source, to in inward]
            both = entering is not None and leaving is not None
            if both and self.held[entering].shape == self.held[leaving].shape:
                self.plan.append((hop, entering, leaving, inward + outward))
                values.append(
                    jnp.where(self.outer(hop), self.held[entering], self.held[leaving])
                )
                continue
            if entering is not None:
                self.plan.append((hop, entering, None, inward))
                values.append(self.held[entering])
            if leaving is not None:
                self.plan.append((hop, None, leaving, outward))
                values.append(self.held[leaving])
        crossing = at.get(self.hops)
        if crossing is not None:
            self.plan.append(
                (None, crossing, None, [(self.hops, self.hops + 1), (self.hops + 1, self.hops)])
            )
            values.append(self.held[crossing])
        return values

    def move(self, values):
        return [lax.ppermute(value, "ctx", pairs) for value, (_, _, _, pairs) in zip(values, self.plan)]

    def absorb(self, values):
        for value, (hop, entering, leaving, _) in zip(values, self.plan):
            if entering is not None:
                self.held[entering] = low(add_up(self.held[entering], value))
            if leaving is not None:
                self.held[leaving] = jnp.where(self.outer(hop), value, self.held[leaving])
        for item, stage in enumerate(self.stage):
            if stage is not None:
                self.stage[item] = stage + 1 if stage < 2 * self.hops else None


def weight_kernel(fresh, *refs):
    first, second, first_rows, second_rows = refs[:4]
    half = first.shape[0] // 2
    total = matmul_plain(first[...], first_rows[...]) + matmul_plain(second[...], second_rows[...])
    if fresh:
        upper, lower = refs[4:]
        upper[...] = low(total[:half])
        lower[...] = low(total[half:])
    else:
        upper_in, lower_in, upper, lower = refs[4:]
        upper[...] = low(total[:half] + upper_in[...].astype(jnp.float32))
        lower[...] = low(total[half:] + lower_in[...].astype(jnp.float32))


def weight_sums(lefts, rights, place, held):
    rows = lefts[0].shape[0] // 2
    depth, width = rights[0].shape
    tile = 512 if width % 512 == 0 else width
    part = jax.ShapeDtypeStruct((rows // 2, width), jnp.bfloat16)
    part_spec = pl.BlockSpec((rows // 2, tile), lambda j: (0, j))
    return pl.pallas_call(
        functools.partial(weight_kernel, held is None),
        grid=(width // tile,),
        in_specs=[pl.BlockSpec((rows, depth), lambda j: (place, 0))] * 2
        + [pl.BlockSpec((depth, tile), lambda j: (0, j))] * 2
        + ([] if held is None else [part_spec] * 2),
        out_specs=[part_spec] * 2,
        out_shape=[part] * 2,
        compiler_params=pltpu.CompilerParams(
            dimension_semantics=("arbitrary",), vmem_limit_bytes=40 * 2**20
        ),
        cost_estimate=pl.CostEstimate(
            flops=4 * rows * depth * width,
            bytes_accessed=4 * (rows * depth + depth * width + rows * width),
            transcendentals=0,
        ),
        name="weight_sums",
    )(*lefts, *rights, *(held or ()))


def spread_line(rows):
    count = lax.axis_size("ctx")
    return [rows] + [
        lax.ppermute(rows, "ctx", [(i, (i + k) % count) for i in range(count)])
        for k in range(1, count)
    ]


def collect_line(parts):
    count = lax.axis_size("ctx")
    rows = parts.shape[0] // count
    total = parts[:rows].astype(jnp.float32)
    for k in range(1, count):
        got = lax.ppermute(
            low(parts[k * rows : (k + 1) * rows]), "ctx", [(i, (i - k) % count) for i in range(count)]
        )
        total = total + got.astype(jnp.float32)
    return total


def pad_columns(values, width):
    return jnp.pad(values, ((0, 0), (0, width - values.shape[1])))


def up_to(width):
    return (width + 127) // 128 * 128


def body(
    activations,
    cotangent,
    seq_length,
    block_order,
    attn_norm,
    query_down,
    query_norm,
    query_up,
    latent_down,
    latent_norm,
    latent_up,
    attn_out,
    mlp_norm,
    gate_weight,
    up_weight,
    down_weight,
):
    ctx_count = lax.axis_size("ctx")
    ctx_place = lax.axis_index("ctx")
    batches = activations.shape[1]
    local_rows = activations.shape[2]
    width = activations.shape[3]
    seq_rows = local_rows * ctx_count
    blocks = block_order.shape[0]
    block_size = seq_rows // blocks
    quads = query_up.shape[1] // (QUAD * (DN + DR))
    query_rank = query_down.shape[1]
    down_width = query_rank + KVR + DR
    bits = chip_bits()

    every_row = jnp.arange(seq_rows, dtype=jnp.int32)
    block_of = every_row // block_size
    placed = jnp.sum(
        jnp.where(
            block_of[:, None] == jnp.arange(blocks, dtype=jnp.int32)[None, :],
            block_order[None, :],
            0,
        ),
        axis=1,
    )
    stored_pos = placed * block_size + every_row % block_size
    near_pos = [
        lax.dynamic_slice_in_dim(
            stored_pos, (ctx_place - k) % ctx_count * local_rows, local_rows
        )
        for k in range(ctx_count)
    ]
    query_pos = near_pos[0]
    key_pos = jnp.concatenate(near_pos)
    local_cos, local_sin = rope_tables(query_pos, DR)
    half = DR // 2
    nothing = jnp.zeros_like(local_sin[:, :half])
    quad_cos = jnp.tile(local_cos, (1, QUAD))
    quad_ahead = jnp.tile(jnp.concatenate([-local_sin[:, :half], nothing], axis=1), (1, QUAD))
    quad_behind = jnp.tile(jnp.concatenate([nothing, local_sin[:, :half]], axis=1), (1, QUAD))
    lengths = seq_length[0]
    allowed = (key_pos[None, :, None] <= query_pos[None, None, :]) & (
        key_pos[None, :, None] < lengths[:, None, None]
    )
    bias = jnp.where(allowed, 0.0, lowest_score).astype(jnp.float32)

    shard_rows = query_down.shape[0]
    column = lambda gain: jnp.pad(gain[:, None], ((0, shard_rows - gain.shape[0]), (0, 0)))
    down_shard = pad_columns(
        jnp.concatenate(
            [query_down, latent_down]
            + [column(gain) for gain in (attn_norm, mlp_norm, query_norm, latent_norm)],
            axis=1,
        ),
        up_to(down_width + 4),
    )
    by_quad = query_up.reshape(-1, quads, QUAD, DN + DR)
    query_shard = jnp.concatenate(
        [
            by_quad[..., :DN].reshape(-1, quads, QUAD * DN),
            by_quad[..., DN:].reshape(-1, quads, QUAD * DR),
        ],
        axis=2,
    ).reshape(query_up.shape)
    by_head = latent_up.reshape(-1, H, DN + DV)
    latent_shard = jnp.concatenate(
        [by_head[..., :DN].reshape(-1, H * DN), by_head[..., DN:].reshape(-1, H * DV)], axis=1
    )
    out_half = attn_out.shape[0] // 2
    one_way = tuple(bits)
    other_way = tuple(bits[::-1])
    hold = lax.optimization_barrier
    rows = batches * local_rows
    lengths_live = query_pos[None, :] < lengths[:, None]
    live = lengths_live.astype(jnp.float32)[..., None]
    out_grad = cotangent[0].astype(jnp.float32) * live
    key_shard, value_shard = latent_shard[:, : H * DN], latent_shard[:, H * DN :]
    upper_out, lower_out = attn_out[:out_half], attn_out[out_half:]
    half_rows = local_rows // 2

    wave = (down_shard, key_shard, query_shard, value_shard)
    ways = (one_way, one_way, other_way, other_way)
    partner_weights = [flip(weight, 1) for weight in (gate_weight, up_weight, down_weight)]
    for place in range(len(bits)):
        moved = [flip(held, way[place]) for held, way in zip(wave, ways)]
        if place == 0:
            branch_grad = low(branch_scale * out_grad)
            moved, branch_grad, upper_out, lower_out = hold((moved, branch_grad, upper_out, lower_out))
        else:
            moved = hold(moved)
        wave = [jnp.concatenate([held, got]) for held, got in zip(wave, moved)]
        wave, branch_grad, upper_out, lower_out = hold((wave, branch_grad, upper_out, lower_out))
    crossed = [flip(held, 1) for held in wave]
    out_wave = (upper_out, lower_out)
    out_ways = (one_way, other_way)
    out_moved = [flip(held, way[0]) for held, way in zip(out_wave, out_ways)]
    crossed, wave = hold((crossed, wave))
    full_down, full_key, full_query, full_value = place_shards(
        [[(held, other, way)] for held, other, way in zip(wave, crossed, ways)]
    )
    gains = full_down[:, down_width : down_width + 4].astype(jnp.float32).T
    devices = lax.axis_size("fsdp")
    spread_gain = lambda gain, size: gain.reshape(devices, -1)[:, : size // devices].reshape(-1)
    attn_gain = gains[0]
    mlp_gain = gains[1]
    query_gain = spread_gain(gains[2], query_rank)
    latent_gain = spread_gain(gains[3], KVR)

    flat_inputs = activations[0].astype(jnp.float32).reshape(rows, width)
    first_normed, first_plain, first_inverse = rms_scale(flat_inputs, attn_gain)
    first_low = low(first_normed)
    down_raw = matmul_plain(first_low, full_down)
    query_mixed, query_plain, query_inverse = rms_scale(down_raw[:, :query_rank], query_gain)
    query_low = low(query_mixed)
    latent_raw = down_raw[:, query_rank:down_width]
    latent_mixed, latent_plain, latent_inverse = rms_scale(latent_raw[:, :KVR], latent_gain)
    both_cos = jnp.tile(local_cos, (batches, 1))
    both_sin = jnp.tile(local_sin, (batches, 1))
    key_rope_low = low(rope_apply(latent_raw[:, KVR:], both_cos, both_sin))
    near_own = jnp.concatenate([low(latent_mixed), key_rope_low], axis=1).reshape(
        batches, local_rows, KVR + DR
    )
    near_own, query_low, out_moved = hold((near_own, query_low, out_moved))
    near = spread_line(near_own)
    out_wave = [jnp.concatenate([held, got]) for held, got in zip(out_wave, out_moved)]
    near, out_wave, branch_grad = hold((near, out_wave, branch_grad))
    for place in range(1, len(bits) - 1):
        out_moved = [flip(held, way[place]) for held, way in zip(out_wave, out_ways)]
        out_wave = [jnp.concatenate([held, got]) for held, got in zip(out_wave, out_moved)]
    out_moved = [flip(held, way[-1]) for held, way in zip(out_wave, out_ways)]
    grad_wave = [branch_grad[None, :, :half_rows], branch_grad[None, :, half_rows:]]
    grad_moved = [flip(held, way[0]) for held, way in zip(grad_wave, out_ways)]
    near = jnp.stack(near, axis=1).reshape(batches, seq_rows, KVR + DR)
    latent_all = near[..., :KVR]
    key_rope_all = near[..., KVR:]
    quad_rope = jnp.tile(key_rope_all, (1, 1, QUAD))
    query_turned, mixed, log_total = attend_forward(
        query_low.reshape(batches, local_rows, query_rank),
        latent_all,
        quad_rope,
        bias,
        quad_cos,
        quad_ahead,
        quad_behind,
        full_query,
        full_key,
        full_value,
        quads,
    )
    out_moved, mixed, grad_wave, grad_moved = hold((out_moved, mixed, grad_wave, grad_moved))
    out_wave = [jnp.concatenate([held, got]) for held, got in zip(out_wave, out_moved)]
    out_crossed = [flip(held, 1) for held in out_wave]
    for place in range(1, len(bits)):
        grad_wave = [jnp.concatenate([held, got]) for held, got in zip(grad_wave, grad_moved)]
        grad_moved = [flip(held, way[place]) for held, way in zip(grad_wave, out_ways)]
    gate_all, up_all, down_all = (
        jnp.concatenate([weight, other])
        for weight, other in zip((gate_weight, up_weight, down_weight), partner_weights)
    )
    out_wave, out_crossed, gate_all, up_all, down_all = hold(
        (out_wave, out_crossed, gate_all, up_all, down_all)
    )
    (full_out,) = place_shards(
        [[(held, other, way) for held, other, way in zip(out_wave, out_crossed, out_ways)]]
    )
    mixed_flat = mixed.reshape(rows, H * DV)
    resid = flat_inputs + branch_scale * matmul_plain(mixed_flat, full_out)
    second_normed, second_plain, second_inverse = rms_scale(resid, mlp_gain)
    second_low = low(second_normed).reshape(batches, local_rows, width)
    of_batch = lambda values, batch: values[batch * local_rows : (batch + 1) * local_rows]
    second_low, grad_wave, grad_moved = hold((second_low, grad_wave, grad_moved))

    def start_rows(batch):
        return [second_low[batch, :half_rows], second_low[batch, half_rows:]]

    def spread_rows(wave, place):
        return [flip(held, way[place]) for held, way in zip(wave, out_ways)]

    def join_rows(wave, moved):
        return [jnp.concatenate([held, got]) for held, got in zip(wave, moved)]

    rows_wave = [start_rows(batch) for batch in range(batches)]
    rows_moved = spread_rows(rows_wave[0], 0)
    grad_wave = join_rows(grad_wave, grad_moved)
    grads_all = [
        jnp.concatenate(
            [held[:, batch].reshape(-1, width) for held in grad_wave]
        )
        for batch in range(batches)
    ]
    hidden_grads = [matmul_right(down_all, grads_all[0])]
    rows_moved, grads_all, hidden_grads = hold((rows_moved, grads_all, hidden_grads))
    rows_wave[0] = join_rows(rows_wave[0], rows_moved)
    for place in range(1, len(bits) - 1):
        rows_wave[0] = join_rows(rows_wave[0], spread_rows(rows_wave[0], place))
    rows_moved = spread_rows(rows_wave[0], -1)
    hidden_grads.append(matmul_right(down_all, grads_all[1]))
    rows_moved, hidden_grads, rows_wave = hold((rows_moved, hidden_grads, rows_wave))
    rows_all = [jnp.concatenate(join_rows(rows_wave[0], rows_moved))]

    def ffn_gate(batch):
        return matmul_right(gate_all, rows_all[batch])

    def ffn_up(batch, gate_value):
        up_value = matmul_right(up_all, rows_all[batch])
        sigmoid_gate = jax.nn.sigmoid(gate_value)
        silu_gate = gate_value * sigmoid_gate
        hidden_low = low(silu_gate * up_value)
        gate_grad = low(
            hidden_grads[batch]
            * up_value
            * sigmoid_gate
            * (1.0 + gate_value * (1.0 - sigmoid_gate))
        )
        up_grad = low(hidden_grads[batch] * silu_gate)
        return hidden_low, gate_grad, up_grad

    def scatter_first(parts):
        quarter = parts.shape[0] // 4
        first, second = parts[: 2 * quarter], parts[2 * quarter :]
        return (
            [first[:quarter], second[:quarter]],
            [flip(first[quarter:], bits[-1]), flip(second[quarter:], bits[0])],
        )

    def scatter_next(kept, got, place):
        joined = [low(add_up(held, value)) for held, value in zip(kept, got)]
        half = joined[0].shape[0] // 2
        moved = [
            flip(joined[0][half:], bits[-1 - place]),
            flip(joined[1][half:], bits[place]),
        ]
        return [held[:half] for held in joined], moved

    def scatter_mid(kept, got):
        for place in range(1, len(bits) - 1):
            kept, got = scatter_next(kept, got, place)
        return scatter_next(kept, got, len(bits) - 1)

    def scatter_end(kept, got):
        return jnp.concatenate([add_up(held, value) for held, value in zip(kept, got)])

    rows_moved = spread_rows(rows_wave[1], 0)
    gate_value = ffn_gate(0)
    rows_moved, gate_value, rows_all = hold((rows_moved, gate_value, rows_all))
    rows_wave[1] = join_rows(rows_wave[1], rows_moved)
    for place in range(1, len(bits) - 1):
        rows_wave[1] = join_rows(rows_wave[1], spread_rows(rows_wave[1], place))
    rows_moved = spread_rows(rows_wave[1], -1)
    ffn_parts = [ffn_up(0, gate_value)]
    branch_part = low(matmul_left(ffn_parts[0][0], down_all))
    rows_moved, ffn_parts, branch_part, rows_wave[1] = hold(
        (rows_moved, ffn_parts, branch_part, rows_wave[1])
    )
    rows_all.append(jnp.concatenate(join_rows(rows_wave[1], rows_moved)))
    first_out = scatter_first(branch_part)
    gate_value = ffn_gate(1)
    first_out, gate_value, rows_all = hold((first_out, gate_value, rows_all))
    first_out = scatter_mid(*first_out)
    ffn_parts.append(ffn_up(1, gate_value))
    first_out, ffn_parts = hold((first_out, ffn_parts))

    def rows_grad_of(batch):
        return low(
            matmul_left(ffn_parts[batch][1], gate_all) + matmul_left(ffn_parts[batch][2], up_all)
        )

    outputs = [low(of_batch(resid, 0) + branch_scale * scatter_end(*first_out))]
    rows_grad = rows_grad_of(0)
    outputs, rows_grad, ffn_parts = hold((outputs, rows_grad, ffn_parts))
    first_grad_way = scatter_first(rows_grad)
    gate_grads = [parts[1] for parts in ffn_parts]
    up_grads = [parts[2] for parts in ffn_parts]
    hiddens = [parts[0] for parts in ffn_parts]
    jobs = [(hiddens, grads_all), (gate_grads, rows_all), (up_grads, rows_all)]
    away = [weight_sums(lefts, rights, 1, None) for lefts, rights in jobs]
    first_grad_way, away, ffn_parts = hold((first_grad_way, away, ffn_parts))
    first_grad_way = scatter_mid(*first_grad_way)
    back = [[flip(part, 1) for part in parts] for parts in away]
    branch_part = low(matmul_left(ffn_parts[1][0], down_all))
    first_grad_way, back, branch_part = hold((first_grad_way, back, branch_part))
    second_out = scatter_first(branch_part)
    own = [weight_sums(*jobs[i], 0, back[i]) for i in range(1)]
    line = LineSum()
    line.add(*own[0])
    sends, second_out, first_grad_way, ffn_parts = hold(
        (line.sends(), second_out, first_grad_way, ffn_parts)
    )

    got = line.move(sends)
    second_out = scatter_mid(*second_out)
    own += [weight_sums(*jobs[i], 0, back[i]) for i in range(1, 3)]
    rows_grad = rows_grad_of(1)
    got, own, rows_grad, second_out = hold((got, own, rows_grad, second_out))
    line.absorb(got)
    line.add(*own[1], *own[2])

    def grads_begin(batch, second_grad):
        second_back, mlp_gain_grad = rms_back(
            second_grad, of_batch(second_plain, batch), of_batch(second_inverse, batch), mlp_gain
        )
        resid_grad = out_grad[batch] + second_back
        attn_grad = low(branch_scale * resid_grad)
        mixed_grad = low(matmul_right(attn_grad, full_out))
        return resid_grad, attn_grad, mixed_grad, mlp_gain_grad

    def grads_attend(batch, mixed_grad):
        query_raw_grad, key_up_part, value_up_part, latent_grad_all, rope_grad_all = attend_backward(
            query_turned[batch],
            mixed_grad,
            latent_all[batch],
            latent_all[batch].T,
            quad_rope[batch],
            key_rope_all[batch].T,
            bias[batch],
            log_total[batch],
            local_cos[:, :half].T,
            local_sin[:, :half].T,
            full_key,
            full_value,
            quads,
        )
        key_rope_grad = rope_grad_all.reshape(seq_rows, QUAD, DR).sum(axis=1)
        latent_part = low(jnp.concatenate([latent_grad_all, key_rope_grad], axis=1))
        return query_raw_grad, key_up_part, value_up_part, latent_part

    def grads_end(batch, query_raw_grad, collected, resid_grad):
        latent_back, latent_gain_grad = rms_back(
            collected[:, :KVR], of_batch(latent_plain, batch), of_batch(latent_inverse, batch), latent_gain
        )
        latent_raw_grad = low(
            jnp.concatenate(
                [latent_back, rope_back(collected[:, KVR:], local_cos, local_sin)], axis=-1
            )
        )
        query_mixed_grad = matmul_right(query_raw_grad, full_query)
        query_back, query_gain_grad = rms_back(
            query_mixed_grad, of_batch(query_plain, batch), of_batch(query_inverse, batch), query_gain
        )
        down_grad = pad_columns(
            jnp.concatenate([low(query_back), latent_raw_grad], axis=1), full_down.shape[1]
        )
        first_grad = matmul_right(down_grad, full_down)
        first_back, attn_gain_grad = rms_back(
            first_grad, of_batch(first_plain, batch), of_batch(first_inverse, batch), attn_gain
        )
        return low(resid_grad + first_back), down_grad, attn_gain_grad, query_gain_grad, latent_gain_grad

    sends, rows_grad, first_grad_way, second_out = hold(
        (line.sends(), rows_grad, first_grad_way, second_out)
    )
    got = line.move(sends)
    second_grad_way = scatter_first(rows_grad)
    begun = [grads_begin(0, scatter_end(*first_grad_way))]
    outputs.append(low(of_batch(resid, 1) + branch_scale * scatter_end(*second_out)))
    got, begun, second_grad_way, outputs = hold((got, begun, second_grad_way, outputs))
    line.absorb(got)

    sends, second_grad_way, begun = hold((line.sends(), second_grad_way, begun))
    got = line.move(sends)
    second_grad_way = scatter_mid(*second_grad_way)
    attended = [grads_attend(0, begun[0][2])]
    got, attended, second_grad_way, begun = hold((got, attended, second_grad_way, begun))
    line.absorb(got)

    sends, second_grad_way, attended = hold((line.sends(), second_grad_way, attended))
    got = line.move(sends)
    begun.append(grads_begin(1, scatter_end(*second_grad_way)))
    collected = [collect_line(attended[0][3])]
    out_sum = low(matmul_left(mixed_flat, jnp.concatenate([begun[0][1], begun[1][1]])))
    got, begun, collected, out_sum = hold((got, begun, collected, out_sum))
    line.absorb(got)
    in_shards = lambda values: values.reshape(devices, -1, values.shape[-1])
    back_way = [1] + bits[::-1]
    back_other = [1] + bits
    out_sum = in_shards(out_sum)
    out_steps = [
        ScatterWhole(out_sum[:, :out_half], back_way),
        ScatterWhole(out_sum[:, out_half:], back_other),
    ]

    sends, begun, out_sends, attended = hold(
        (line.sends(), begun, [job.send() for job in out_steps], attended)
    )
    got = line.move(sends)
    out_got = [job.move(value) for job, value in zip(out_steps, out_sends)]
    attended.append(grads_attend(1, begun[1][2]))
    got, attended, out_got = hold((got, attended, out_got))
    line.absorb(got)
    for job, value in zip(out_steps, out_got):
        job.absorb(value)

    sends, attended, out_sends = hold(
        (line.sends(), attended, [job.send() for job in out_steps])
    )
    got = line.move(sends)
    out_got = [job.move(value) for job, value in zip(out_steps, out_sends)]
    collected.append(collect_line(attended[1][3]))
    latent_up_sum = low(
        jnp.concatenate([attended[0][1] + attended[1][1], attended[0][2] + attended[1][2]], axis=1)
    )
    query_sum = low(matmul_left(query_low, jnp.concatenate([attended[0][0], attended[1][0]])))
    ended = [
        grads_end(batch, attended[batch][0], collected[batch], begun[batch][0])
        for batch in range(batches)
    ]
    input_grads = [ended[batch][0] for batch in range(batches)]
    gain_sums = [
        ended[0][2] + ended[1][2],
        begun[0][3] + begun[1][3],
        ended[0][3] + ended[1][3],
        ended[0][4] + ended[1][4],
    ]
    places = lax.broadcasted_iota(jnp.int32, full_down.shape, 1) - down_width
    down_sum = matmul_left(first_low, jnp.concatenate([ended[0][1], ended[1][1]]))
    gathered_gain = lambda gain: jnp.pad(
        gain.reshape(devices, -1), ((0, 0), (0, shard_rows - gain.shape[0] // devices))
    ).reshape(-1)
    gain_columns = gain_sums[:2] + [gathered_gain(gain) for gain in gain_sums[2:]]
    for place, gain in enumerate(gain_columns):
        down_sum = jnp.where(places == place, gain[:, None], down_sum)
    down_sum = low(down_sum)
    got, out_got, latent_up_sum, query_sum, down_sum = hold(
        (got, out_got, latent_up_sum, query_sum, down_sum)
    )
    line.absorb(got)
    for job, value in zip(out_steps, out_got):
        job.absorb(value)

    steps = [
        ScatterWhole(in_shards(down_sum), back_way),
        ScatterWhole(in_shards(query_sum), back_other),
        ScatterWhole(in_shards(latent_up_sum), back_way),
    ]
    while line.busy() or steps:
        jobs = [job for job in out_steps + steps if job.order]
        sends, values = hold((line.sends(), [job.send() for job in jobs]))
        got = line.move(sends)
        values = [job.move(value) for job, value in zip(jobs, values)]
        got, values = hold((got, values))
        line.absorb(got)
        for job, value in zip(jobs, values):
            job.absorb(value)
        if out_steps and not any(job.order for job in out_steps):
            line.add(jnp.concatenate([job.held[0] for job in out_steps]))
            out_steps = []
        if steps and not any(job.order for job in steps):
            line.add(*[job.held[0] for job in steps])
            steps = []
    totals = [total.astype(jnp.float32) for total in line.held]
    ffn_totals = [jnp.concatenate(totals[2 * i : 2 * i + 2]) for i in (1, 2, 0)]
    out_total, down_total, query_total, latent_total = totals[6:]
    by_quad = query_total.reshape(-1, quads, QUAD * (DN + DR))
    query_up_total = jnp.concatenate(
        [
            by_quad[..., : QUAD * DN].reshape(-1, quads, QUAD, DN),
            by_quad[..., QUAD * DN :].reshape(-1, quads, QUAD, DR),
        ],
        axis=-1,
    ).reshape(query_up.shape)
    latent_up_total = jnp.concatenate(
        [
            latent_total[:, : H * DN].reshape(-1, H, DN),
            latent_total[:, H * DN :].reshape(-1, H, DV),
        ],
        axis=-1,
    ).reshape(latent_up.shape)
    return (
        jnp.stack(outputs)[None],
        jnp.stack(input_grads)[None],
        down_total[:, down_width],
        down_total[:, :query_rank],
        down_total[: query_norm.shape[0], down_width + 2],
        query_up_total,
        down_total[:, query_rank:down_width],
        down_total[: latent_norm.shape[0], down_width + 3],
        latent_up_total,
        out_total,
        down_total[:, down_width + 1],
        ffn_totals[0],
        ffn_totals[1],
        ffn_totals[2],
    )


def solution(mesh):
    placed = (
        P("fsdp", None, "ctx", None),
        P("fsdp", None, "ctx", None),
        P("fsdp", None),
        P(),
        P("fsdp"),
        P("fsdp", None),
        P("fsdp"),
        P("fsdp", None),
        P("fsdp", None),
        P("fsdp"),
        P("fsdp", None),
        P("fsdp", None),
        P("fsdp"),
        P("fsdp", None),
        P("fsdp", None),
        P("fsdp", None),
    )
    return jax.shard_map(
        body,
        mesh=mesh,
        in_specs=placed,
        out_specs=(
            P("fsdp", None, "ctx", None),
            P("fsdp", None, "ctx", None),
            P("fsdp"),
            P("fsdp", None),
            P("fsdp"),
            P("fsdp", None),
            P("fsdp", None),
            P("fsdp"),
            P("fsdp", None),
            P("fsdp", None),
            P("fsdp"),
            P("fsdp", None),
            P("fsdp", None),
            P("fsdp", None),
        ),
        check_vma=False,
    )
```

```python
import functools
import math

import jax
import jax.numpy as jnp
from jax import lax
from jax.experimental import pallas as pl
from jax.experimental.pallas import tpu as pltpu
from jax.sharding import PartitionSpec as P

H = 40
DN = 64
DR = 32
DV = 64
KVR = 256
QUAD = 4


branch_scale = 1.4 / math.sqrt(62.0)
norm_eps = 1e-05
rope_base = 10000.0
lowest_score = -1e30
score_scale = (DN + DR) ** -0.5
exp_scale = math.log2(math.e) * score_scale


def rms_scale(values, gain):
    inverse = lax.rsqrt(jnp.mean(values * values, axis=-1, keepdims=True) + norm_eps)
    plain = values * inverse
    return (plain * gain, plain, inverse)


def rms_back(grad_out, plain, inverse, gain):
    gain_grad = jnp.sum(grad_out * plain, axis=0)
    scaled = grad_out * gain
    values_grad = inverse * (scaled - plain * jnp.mean(scaled * plain, axis=-1, keepdims=True))
    return (values_grad, gain_grad)


def rope_tables(positions, width):
    half = width // 2
    freq = rope_base ** (-(jnp.arange(half, dtype=jnp.float32) * 2.0 / width))
    angle = positions.astype(jnp.float32)[:, None] * freq[None, :]
    return (
        jnp.concatenate([jnp.cos(angle), jnp.cos(angle)], axis=-1),
        jnp.concatenate([jnp.sin(angle), jnp.sin(angle)], axis=-1),
    )


def turn_half(values):
    half = values.shape[-1] // 2
    return jnp.concatenate([-values[..., half:], values[..., :half]], axis=-1)


def turn_back(values):
    half = values.shape[-1] // 2
    return jnp.concatenate([values[..., half:], -values[..., :half]], axis=-1)


def rope_apply(values, cosine, sine):
    return values * cosine + turn_half(values) * sine


def rope_back(grads, cosine, sine):
    return grads * cosine + turn_back(grads * sine)


def matmul_plain(left, right):
    return jnp.dot(left, right, preferred_element_type=jnp.float32)


def matmul_left(left, right):
    return lax.dot_general(
        left, right, (((0,), (0,)), ((), ())), preferred_element_type=jnp.float32
    )


def matmul_right(left, right):
    return lax.dot_general(
        left, right, (((1,), (1,)), ((), ())), preferred_element_type=jnp.float32
    )


def flip(values, bit):
    count = lax.axis_size("fsdp")
    return lax.ppermute(values, "fsdp", [(i, i ^ bit) for i in range(count)])


def chip_bits():
    return [1 << k for k in range(1, lax.axis_size("fsdp").bit_length() - 1)]


def low(values):
    return values.astype(jnp.bfloat16)


def add_up(left, right):
    return left.astype(jnp.float32) + right.astype(jnp.float32)


def place_kernel(plan, me_ref, *refs):
    sources, outs, sems = refs[: len(plan)], refs[len(plan) : -1], refs[-1]
    me = me_ref[0]
    copies = []
    for source, (out, rows, places, stride, offset) in zip(sources, plan):
        for k, place in enumerate(places):
            start = pl.multiple_of((me ^ place) * stride + offset, 16)
            copies.append(
                pltpu.make_async_copy(
                    source.at[pl.ds(k * rows, rows)],
                    outs[out].at[pl.ds(start, rows)],
                    sems.at[len(copies)],
                )
            )
    for copy in copies:
        copy.start()
    for copy in copies:
        copy.wait()


def place_shards(groups):
    count = lax.axis_size("fsdp")
    me = lax.axis_index("fsdp").astype(jnp.int32).reshape(1)
    plan, sources, shapes = [], [], []
    for out, parts in enumerate(groups):
        heights = [sum(piece.shape[0] for piece, _ in part) // count for part in parts]
        offset = 0
        for part, rows in zip(parts, heights):
            for piece, places in part:
                plan.append((out, rows, tuple(places), sum(heights), offset))
                sources.append(piece)
            offset += rows
        shapes.append(jax.ShapeDtypeStruct((count * sum(heights), parts[0][0][0].shape[1]), jnp.bfloat16))
    anywhere = pl.BlockSpec(memory_space=pl.ANY)
    return pl.pallas_call(
        functools.partial(place_kernel, tuple(plan)),
        in_specs=[pl.BlockSpec(memory_space=pltpu.SMEM)] + [anywhere] * len(sources),
        out_specs=[pl.BlockSpec(memory_space=pltpu.VMEM)] * len(shapes),
        out_shape=shapes,
        scratch_shapes=[pltpu.SemaphoreType.DMA((sum(len(of[2]) for of in plan),))],
        compiler_params=pltpu.CompilerParams(vmem_limit_bytes=32 * 2**20),
        name="place_shards",
    )(me, *sources)


class ScatterWhole:
    def __init__(self, held, order):
        self.held = held
        self.order = list(order)
        self.left = [1 << k for k in range(held.shape[0].bit_length() - 2, -1, -1)]
        self.me = lax.axis_index("fsdp")

    def send(self):
        rows, width = self.held.shape[1:]
        place = self.left.index(self.order[0])
        below = 1 << (len(self.left) - place - 1)
        held = self.held.reshape(-1, 2, below, rows, width)
        mine = (self.me // self.order[0]) % 2
        self.kept = lax.dynamic_index_in_dim(held, mine, 1, keepdims=False)
        return lax.dynamic_index_in_dim(held, 1 - mine, 1, keepdims=False)

    def move(self, value):
        return flip(value, self.order[0])

    def absorb(self, value):
        self.held = low(add_up(self.kept, value)).reshape((-1,) + self.held.shape[1:])
        self.left.remove(self.order.pop(0))


def lane_part(values, width, place):
    lane = lax.broadcasted_iota(jnp.int32, values.shape, 1)
    return jnp.where(lane // width == place, values, 0.0)


def pair_rows(nope, rope, pair):
    both = nope[:, pair * 2 * DN : (pair + 1) * 2 * DN]
    return low(
        jnp.concatenate(
            [
                jnp.concatenate(
                    [lane_part(both, DN, head), lane_part(rope, DR, 2 * pair + head)], axis=1
                )
                for head in range(2)
            ],
            axis=0,
        )
    )


def forward_kernel(
    low_ref, latent_ref, rope_ref, bias_ref, cos_ref, ahead_ref, behind_ref,
    query_w, key_w, value_w, query_ref, mixed_ref, total_ref,
):
    rows = low_ref.shape[1]
    raw = matmul_plain(low_ref[0], query_w[...])
    nope = raw[:, : QUAD * DN]
    rope = raw[:, QUAD * DN :]
    lanes = QUAD * DR
    rope = (
        rope * cos_ref[...]
        + pltpu.roll(rope, lanes - DR // 2, 1) * ahead_ref[...]
        + pltpu.roll(rope, DR // 2, 1) * behind_ref[...]
    )
    query_ref[0] = low(jnp.concatenate([nope, rope], axis=1))
    latent = latent_ref[0]
    keys = low(matmul_plain(latent, key_w[...]))
    values = low(matmul_plain(latent, value_w[...])).T
    mixed = []
    for pair in range(2):
        key_cat = jnp.concatenate(
            [keys[:, pair * 2 * DN : (pair + 1) * 2 * DN], rope_ref[0]], axis=1
        )
        scores = matmul_right(key_cat, pair_rows(nope, rope, pair))
        for head in range(2):
            place = 2 * pair + head
            own = scores[:, head * rows : (head + 1) * rows] * exp_scale + bias_ref[0]
            top = jnp.max(own, axis=0, keepdims=True)
            expo = jnp.exp2(own - top)
            total = jnp.sum(expo, axis=0, keepdims=True)
            out = matmul_plain(values[place * DV : (place + 1) * DV], low(expo))
            mixed.append(out / total)
            total_ref[0, 0, place : place + 1, :] = top + jnp.log2(total)
    mixed_ref[0] = low(jnp.concatenate(mixed, axis=0).T)


def attend_forward(query_low, latent, rope_keys, bias, cosine, ahead, behind, query_w, latent_w, quads):
    batches, rows, rank = query_low.shape
    keys, width = latent.shape[1:]
    qw, kw, rw = QUAD * (DN + DR), QUAD * DN, QUAD * DR
    fixed = lambda b, j: (0, 0)
    whole = lambda b, j: (b, 0, 0)
    flops = batches * quads * (2 * keys * width * 2 * kw + 2 * rows * rank * qw + 4 * 4 * keys * rows * 256)
    return pl.pallas_call(
        forward_kernel,
        grid=(batches, quads),
        in_specs=[
            pl.BlockSpec((1, rows, rank), whole),
            pl.BlockSpec((1, keys, width), whole),
            pl.BlockSpec((1, keys, rw), whole),
            pl.BlockSpec((1, keys, rows), whole),
            pl.BlockSpec((rows, rw), fixed),
            pl.BlockSpec((rows, rw), fixed),
            pl.BlockSpec((rows, rw), fixed),
            pl.BlockSpec((rank, qw), lambda b, j: (0, j)),
            pl.BlockSpec((width, kw), lambda b, j: (0, j)),
            pl.BlockSpec((width, kw), lambda b, j: (0, quads + j)),
        ],
        out_specs=[
            pl.BlockSpec((1, rows, qw), lambda b, j: (b, 0, j)),
            pl.BlockSpec((1, rows, kw), lambda b, j: (b, 0, j)),
            pl.BlockSpec((1, 1, QUAD, rows), lambda b, j: (b, j, 0, 0)),
        ],
        out_shape=[
            jax.ShapeDtypeStruct((batches, rows, quads * qw), jnp.bfloat16),
            jax.ShapeDtypeStruct((batches, rows, quads * kw), jnp.bfloat16),
            jax.ShapeDtypeStruct((batches, quads, QUAD, rows), jnp.float32),
        ],
        compiler_params=pltpu.CompilerParams(
            dimension_semantics=("arbitrary", "arbitrary"), vmem_limit_bytes=48 * 2**20
        ),
        cost_estimate=pl.CostEstimate(
            flops=int(flops), bytes_accessed=40 * 2**20, transcendentals=batches * quads * 4 * keys * rows
        ),
        name="attend_forward",
    )(query_low, latent, rope_keys, bias, cosine, ahead, behind, query_w, latent_w, latent_w)


def backward_kernel(
    query_ref, grad_ref, latent_ref, flat_ref, rope_ref, turned_ref, bias_ref, total_ref,
    cos_ref, sin_ref, key_w, value_w,
    query_out, key_up_out, value_up_out, latent_out, rope_out,
):
    rows = query_ref.shape[0]
    half = DR // 2

    @pl.when(pl.program_id(0) == 0)
    def _():
        latent_out[...] = jnp.zeros_like(latent_out)
        rope_out[...] = jnp.zeros_like(rope_out)

    latent = latent_ref[...]
    keys = low(matmul_plain(latent, key_w[...]))
    values = low(matmul_plain(latent, value_w[...]))
    turned_keys = keys.T
    query = query_ref[...].astype(jnp.float32)
    nope = query[:, : QUAD * DN]
    rope = query[:, QUAD * DN :]
    grad = grad_ref[...].astype(jnp.float32)
    key_grads, value_grads, nope_grads, rope_grads = [], [], [], []
    for pair in range(2):
        lanes = slice(pair * 2 * DN, (pair + 1) * 2 * DN)
        key_cat = jnp.concatenate([keys[:, lanes], rope_ref[...]], axis=1)
        query_cat = pair_rows(nope, rope, pair)
        grad_cat = low(
            jnp.concatenate([lane_part(grad[:, lanes], DV, head) for head in range(2)], axis=0)
        )
        scores = matmul_right(key_cat, query_cat)
        prob_grads = matmul_right(values[:, lanes], grad_cat)
        probs_low, score_low = [], []
        for head in range(2):
            place = 2 * pair + head
            cut = slice(head * rows, (head + 1) * rows)
            probs = jnp.exp2(
                scores[:, cut] * exp_scale + bias_ref[...] - total_ref[0, place : place + 1, :]
            )
            mixed = probs * prob_grads[:, cut]
            dots = jnp.sum(mixed, axis=0, keepdims=True)
            score_grad = low(mixed - probs * dots)
            probs_low.append(low(probs))
            score_low.append(score_grad)
            left = jnp.concatenate(
                [turned_keys[place * DN : (place + 1) * DN], turned_ref[...]], axis=0
            )
            turned = matmul_plain(left, score_grad) * score_scale
            nope_grads.append(turned[:DN])
            upper, lower = turned[DN : DN + half], turned[DN + half :]
            rope_grads.append(upper * cos_ref[...] + lower * sin_ref[...])
            rope_grads.append(lower * cos_ref[...] - upper * sin_ref[...])
        value_grads.append(matmul_plain(jnp.concatenate(probs_low, axis=1), grad_cat))
        key_cat_grad = matmul_plain(jnp.concatenate(score_low, axis=1), query_cat)
        key_grads.append(key_cat_grad[:, : 2 * DN])
        rope_out[...] += key_cat_grad[:, 2 * DN :] * score_scale
    query_out[...] = low(jnp.concatenate(nope_grads + rope_grads, axis=0).T)
    key_grad = low(jnp.concatenate(key_grads, axis=1) * score_scale)
    value_grad = low(jnp.concatenate(value_grads, axis=1))
    key_up_out[...] = matmul_plain(flat_ref[...], key_grad)
    value_up_out[...] = matmul_plain(flat_ref[...], value_grad)
    latent_out[...] += matmul_right(key_grad, key_w[...]) + matmul_right(value_grad, value_w[...])


def attend_backward(query, grad, latent, latent_flat, rope_keys, rope_flat, bias, totals, cos_flat, sin_flat, latent_w, quads):
    rows = query.shape[0]
    keys, width = latent.shape
    qw, kw, rw = QUAD * (DN + DR), QUAD * DN, QUAD * DR
    fixed = lambda j: (0, 0)
    step = lambda j: (0, j)
    flops = quads * (2 * keys * width * 6 * kw + 5 * 4 * 2 * keys * rows * 256)
    return pl.pallas_call(
        backward_kernel,
        grid=(quads,),
        in_specs=[
            pl.BlockSpec((rows, qw), step),
            pl.BlockSpec((rows, kw), step),
            pl.BlockSpec((keys, width), fixed),
            pl.BlockSpec((width, keys), fixed),
            pl.BlockSpec((keys, rw), fixed),
            pl.BlockSpec((DR, keys), fixed),
            pl.BlockSpec((keys, rows), fixed),
            pl.BlockSpec((1, QUAD, rows), lambda j: (j, 0, 0)),
            pl.BlockSpec((DR // 2, rows), fixed),
            pl.BlockSpec((DR // 2, rows), fixed),
            pl.BlockSpec((width, kw), step),
            pl.BlockSpec((width, kw), lambda j: (0, quads + j)),
        ],
        out_specs=[
            pl.BlockSpec((rows, qw), step),
            pl.BlockSpec((width, kw), step),
            pl.BlockSpec((width, kw), step),
            pl.BlockSpec((keys, width), fixed),
            pl.BlockSpec((keys, rw), fixed),
        ],
        out_shape=[
            jax.ShapeDtypeStruct((rows, quads * qw), jnp.bfloat16),
            jax.ShapeDtypeStruct((width, quads * kw), jnp.float32),
            jax.ShapeDtypeStruct((width, quads * kw), jnp.float32),
            jax.ShapeDtypeStruct((keys, width), jnp.float32),
            jax.ShapeDtypeStruct((keys, rw), jnp.float32),
        ],
        compiler_params=pltpu.CompilerParams(
            dimension_semantics=("arbitrary",), vmem_limit_bytes=48 * 2**20
        ),
        cost_estimate=pl.CostEstimate(
            flops=int(flops), bytes_accessed=25 * 2**20, transcendentals=quads * 4 * keys * rows
        ),
        name="attend_backward",
    )(query, grad, latent, latent_flat, rope_keys, rope_flat, bias, totals, cos_flat, sin_flat, latent_w, latent_w)


class LineSum:
    def __init__(self):
        self.count = lax.axis_size("ctx")
        self.me = lax.axis_index("ctx")
        self.hops = self.count // 2 - 1
        self.held = []
        self.stage = []
        self.queue = []

    def add(self, *pieces):
        for piece in pieces:
            self.queue.append(len(self.held))
            self.held.append(piece)
            self.stage.append(None)

    def busy(self):
        return bool(self.queue) or any(s is not None and s >= 0 for s in self.stage)

    def outer(self, hop):
        return (self.me == hop) | (self.me == self.count - 1 - hop)

    def sends(self):
        if self.queue:
            self.stage[self.queue.pop(0)] = 0
        self.plan, values = [], []
        at = {stage: item for item, stage in enumerate(self.stage) if stage is not None}
        last = self.count - 1
        for hop in range(self.hops):
            entering, leaving = at.get(hop), at.get(2 * self.hops - hop)
            inward = [(hop, hop + 1), (last - hop, last - hop - 1)]
            outward = [(to, source) for source, to in inward]
            both = entering is not None and leaving is not None
            if both and self.held[entering].shape == self.held[leaving].shape:
                self.plan.append((hop, entering, leaving, inward + outward))
                values.append(
                    jnp.where(self.outer(hop), self.held[entering], self.held[leaving])
                )
                continue
            if entering is not None:
                self.plan.append((hop, entering, None, inward))
                values.append(self.held[entering])
            if leaving is not None:
                self.plan.append((hop, None, leaving, outward))
                values.append(self.held[leaving])
        crossing = at.get(self.hops)
        if crossing is not None:
            self.plan.append(
                (None, crossing, None, [(self.hops, self.hops + 1), (self.hops + 1, self.hops)])
            )
            values.append(self.held[crossing])
        return values

    def move(self, values):
        return [lax.ppermute(value, "ctx", pairs) for value, (_, _, _, pairs) in zip(values, self.plan)]

    def absorb(self, values):
        for value, (hop, entering, leaving, _) in zip(values, self.plan):
            if entering is not None:
                self.held[entering] = low(add_up(self.held[entering], value))
            if leaving is not None:
                self.held[leaving] = jnp.where(self.outer(hop), value, self.held[leaving])
        for item, stage in enumerate(self.stage):
            if stage is not None:
                self.stage[item] = stage + 1 if stage < 2 * self.hops else None


def up_kernel(parts, gate_w, up_w, down_w, *refs):
    rows_refs, grad_refs = refs[:parts], refs[parts : 2 * parts]
    hidden_ref, gate_ref, up_ref = refs[2 * parts :]
    start = 0
    for rows_ref, grad_ref in zip(rows_refs, grad_refs):
        cut = slice(start, start + rows_ref.shape[0])
        start += rows_ref.shape[0]
        gate_value = matmul_right(gate_w[...], rows_ref[...])
        up_value = matmul_right(up_w[...], rows_ref[...])
        hidden_grad = matmul_right(down_w[...], grad_ref[...])
        sigmoid_gate = 1.0 / (1.0 + jnp.exp(-gate_value))
        silu_gate = gate_value * sigmoid_gate
        hidden_ref[:, cut] = low(silu_gate * up_value)
        gate_ref[:, cut] = low(
            hidden_grad * up_value * sigmoid_gate * (1.0 + gate_value * (1.0 - sigmoid_gate))
        )
        up_ref[:, cut] = low(hidden_grad * silu_gate)


def hidden_tile(units):
    return max(size for size in range(16, 401, 16) if units % size == 0)


def feed_up(rows_parts, grad_parts, gate_all, up_all, down_all):
    units, width = gate_all.shape
    tile = hidden_tile(units)
    rows = sum(part.shape[0] for part in rows_parts)
    whole = [
        pl.BlockSpec(part.shape, lambda i: (0, 0), pipeline_mode=pl.Buffered(1))
        for part in (*rows_parts, *grad_parts)
    ]
    return pl.pallas_call(
        functools.partial(up_kernel, len(rows_parts)),
        grid=(units // tile,),
        in_specs=[pl.BlockSpec((tile, width), lambda i: (i, 0))] * 3 + whole,
        out_specs=[pl.BlockSpec((tile, rows), lambda i: (i, 0))] * 3,
        out_shape=[jax.ShapeDtypeStruct((units, rows), jnp.bfloat16)] * 3,
        compiler_params=pltpu.CompilerParams(
            dimension_semantics=("arbitrary",), vmem_limit_bytes=52 * 2**20
        ),
        cost_estimate=pl.CostEstimate(
            flops=6 * units * width * rows,
            bytes_accessed=6 * units * width + 4 * rows * width + 6 * units * rows,
            transcendentals=units * rows,
        ),
        name="feed_up",
    )(gate_all, up_all, down_all, *rows_parts, *grad_parts)


def down_kernel(pairs, slots, *refs):
    units, weights = refs[:pairs], refs[pairs : 2 * pairs]
    outs, turned = refs[2 * pairs : -pairs], refs[-pairs:]

    @pl.when(pl.program_id(0) == 0)
    def _():
        for unit_ref, turned_ref in zip(units, turned):
            turned_ref[...] = unit_ref[...].T

    total = matmul_plain(turned[0][...], weights[0][...])
    for place in range(1, pairs):
        total += matmul_plain(turned[place][...], weights[place][...])
    for out, starts in zip(outs, slots):
        step = out.shape[0] // len(starts)
        for place, start in enumerate(starts):
            out[place * step : (place + 1) * step] = low(total[start : start + step])


def feed_down(units, weights, slots):
    parts = len(slots)
    depth, rows = units[0].shape
    width = weights[0].shape[1]
    tile = 512 if width % 512 == 0 else width
    return pl.pallas_call(
        functools.partial(down_kernel, len(units), slots),
        grid=(width // tile,),
        in_specs=[pl.BlockSpec((depth, rows), lambda j: (0, 0), pipeline_mode=pl.Buffered(1))]
        * len(units)
        + [pl.BlockSpec((depth, tile), lambda j: (0, j))] * len(units),
        out_specs=[pl.BlockSpec((rows // parts, tile), lambda j: (0, j))] * parts,
        out_shape=[jax.ShapeDtypeStruct((rows // parts, width), jnp.bfloat16)] * parts,
        scratch_shapes=[pltpu.VMEM((rows, depth), jnp.bfloat16)] * len(units),
        compiler_params=pltpu.CompilerParams(
            dimension_semantics=("arbitrary",), vmem_limit_bytes=48 * 2**20
        ),
        cost_estimate=pl.CostEstimate(
            flops=2 * len(units) * depth * rows * width,
            bytes_accessed=2 * len(units) * depth * (rows + width) + 2 * rows * width,
            transcendentals=0,
        ),
        name="feed_down",
    )(*units, *weights)


def weight_kernel(lefts, counts, fresh, *refs):
    left_refs, right_refs = refs[:lefts], refs[lefts : lefts + sum(counts)]
    half = left_refs[0].shape[0] // 2
    total, start = None, 0
    for left, count in zip(left_refs, counts):
        right = jnp.concatenate([ref[...] for ref in right_refs[start : start + count]], axis=0)
        start += count
        product = matmul_plain(left[...], right)
        total = product if total is None else total + product
    rest = refs[lefts + sum(counts) :]
    if fresh:
        upper, lower = rest
        upper[...] = low(total[:half])
        lower[...] = low(total[half:])
    else:
        upper_in, lower_in, upper, lower = rest
        upper[...] = low(total[:half] + upper_in[...].astype(jnp.float32))
        lower[...] = low(total[half:] + lower_in[...].astype(jnp.float32))


def weight_sums(lefts, rights, place, held):
    rows, depth = lefts[0].shape[0] // 2, lefts[0].shape[1]
    width = rights[0][0].shape[1]
    tile = 512 if width % 512 == 0 else width
    part = jax.ShapeDtypeStruct((rows // 2, width), jnp.bfloat16)
    part_spec = pl.BlockSpec((rows // 2, tile), lambda j: (0, j))
    flat = [piece for pieces in rights for piece in pieces]
    return pl.pallas_call(
        functools.partial(
            weight_kernel, len(lefts), tuple(len(pieces) for pieces in rights), held is None
        ),
        grid=(width // tile,),
        in_specs=[pl.BlockSpec((rows, depth), lambda j: (place, 0))] * len(lefts)
        + [pl.BlockSpec((piece.shape[0], tile), lambda j: (0, j)) for piece in flat]
        + ([] if held is None else [part_spec] * 2),
        out_specs=[part_spec] * 2,
        out_shape=[part] * 2,
        compiler_params=pltpu.CompilerParams(
            dimension_semantics=("arbitrary",), vmem_limit_bytes=40 * 2**20
        ),
        cost_estimate=pl.CostEstimate(
            flops=2 * len(lefts) * rows * depth * width,
            bytes_accessed=2 * len(lefts) * (rows * depth + depth * width) + 2 * rows * width,
            transcendentals=0,
        ),
        name="weight_sums",
    )(*lefts, *flat, *(held or ()))


def pad_columns(values, width):
    return jnp.pad(values, ((0, 0), (0, width - values.shape[1])))


def up_to(width):
    return (width + 127) // 128 * 128


def body(
    activations,
    cotangent,
    seq_length,
    block_order,
    attn_norm,
    query_down,
    query_norm,
    query_up,
    latent_down,
    latent_norm,
    latent_up,
    attn_out,
    mlp_norm,
    gate_weight,
    up_weight,
    down_weight,
):
    ctx_count = lax.axis_size("ctx")
    ctx_place = lax.axis_index("ctx")
    batches = activations.shape[1]
    local_rows = activations.shape[2]
    width = activations.shape[3]
    seq_rows = local_rows * ctx_count
    blocks = block_order.shape[0]
    block_size = seq_rows // blocks
    quads = query_up.shape[1] // (QUAD * (DN + DR))
    query_rank = query_down.shape[1]
    bits = chip_bits()

    every_row = jnp.arange(seq_rows, dtype=jnp.int32)
    block_of = every_row // block_size
    placed = jnp.sum(
        jnp.where(
            block_of[:, None] == jnp.arange(blocks, dtype=jnp.int32)[None, :],
            block_order[None, :],
            0,
        ),
        axis=1,
    )
    stored_pos = placed * block_size + every_row % block_size
    query_pos = lax.dynamic_slice_in_dim(stored_pos, ctx_place * local_rows, local_rows)
    key_pos = stored_pos
    local_cos, local_sin = rope_tables(query_pos, DR)
    half = DR // 2
    nothing = jnp.zeros_like(local_sin[:, :half])
    quad_cos = jnp.tile(local_cos, (1, QUAD))
    quad_ahead = jnp.tile(jnp.concatenate([-local_sin[:, :half], nothing], axis=1), (1, QUAD))
    quad_behind = jnp.tile(jnp.concatenate([nothing, local_sin[:, :half]], axis=1), (1, QUAD))
    lengths = seq_length[0]
    allowed = (key_pos[None, :, None] <= query_pos[None, None, :]) & (
        key_pos[None, :, None] < lengths[:, None, None]
    )
    bias = jnp.where(allowed, 0.0, lowest_score).astype(jnp.float32)

    hold = lax.optimization_barrier
    rows = batches * local_rows
    half_rows = local_rows // 2
    devices = lax.axis_size("fsdp")
    one_way = tuple(bits)
    other_way = tuple(bits[::-1])
    both_ways = (one_way, other_way)
    last = len(bits) - 1

    def depart(wave, ways, place):
        return [flip(held, way[place]) for held, way in zip(wave, ways)]

    def join(wave, moved):
        return [jnp.concatenate([held, got]) for held, got in zip(wave, moved)]

    shard_rows = query_down.shape[0]
    column = lambda gain: jnp.pad(gain[:, None], ((0, shard_rows - gain.shape[0]), (0, 0)))
    gain_place = KVR + DR
    small_shard = pad_columns(
        jnp.concatenate(
            [latent_down] + [column(gain) for gain in (attn_norm, mlp_norm, query_norm, latent_norm)],
            axis=1,
        ),
        up_to(gain_place + 4),
    )
    small_wave = [small_shard[: shard_rows // 2], small_shard[shard_rows // 2 :]]
    small_moved = depart(small_wave, both_ways, 0)
    by_quad = query_up.reshape(-1, quads, QUAD, DN + DR)
    query_shard = jnp.concatenate(
        [
            by_quad[..., :DN].reshape(-1, quads, QUAD * DN),
            by_quad[..., DN:].reshape(-1, quads, QUAD * DR),
        ],
        axis=2,
    ).reshape(query_up.shape)
    by_head = latent_up.reshape(-1, H, DN + DV)
    latent_shard = jnp.concatenate(
        [by_head[..., :DN].reshape(-1, H * DN), by_head[..., DN:].reshape(-1, H * DV)], axis=1
    )
    wave = [query_down, latent_shard, query_shard]
    ways = (one_way, one_way, other_way)
    moved = depart(wave, ways, 0)

    def places_of(way, bit):
        places = [0]
        for step in way[:-1]:
            places = places + [place ^ step for place in places]
        return [place ^ bit for place in places], [place ^ way[-1] ^ bit for place in places]

    def pieces_of(held, got, held_crossed, got_crossed, way):
        pieces = []
        for first, second, bit in ((held, got, 0), (held_crossed, got_crossed, 1)):
            for piece, places in zip((first, second), places_of(way, bit)):
                pieces.append((piece, places))
        return pieces

    small_moved, small_wave = hold((small_moved, small_wave))
    small_wave = join(small_wave, small_moved)
    for place in range(1, last):
        small_wave = join(small_wave, depart(small_wave, both_ways, place))
    small_moved = depart(small_wave, both_ways, last)
    lengths_live = query_pos[None, :] < lengths[:, None]
    live = lengths_live.astype(jnp.float32)[..., None]
    flat_inputs = activations[0].reshape(rows, width)
    inverse = lax.rsqrt(
        jnp.mean(flat_inputs.astype(jnp.float32) ** 2, axis=-1, keepdims=True) + norm_eps
    )
    small_moved, small_wave, inverse, moved, wave = hold(
        (small_moved, small_wave, inverse, moved, wave)
    )
    small_crossed = [flip(held, 1) for held in (*small_wave, *small_moved)]
    wave = join(wave, moved)
    for place in range(1, last):
        wave = join(wave, depart(wave, ways, place))
    small_crossed, small_wave, small_moved, wave = hold(
        (small_crossed, small_wave, small_moved, wave)
    )
    moved = depart(wave, ways, last)
    (full_small,) = place_shards(
        [
            [
                pieces_of(small_wave[i], small_moved[i], small_crossed[i], small_crossed[2 + i], both_ways[i])
                for i in range(2)
            ]
        ]
    )
    gains = full_small[:, gain_place : gain_place + 4].astype(jnp.float32).T
    spread_gain = lambda gain, size: gain.reshape(devices, -1)[:, : size // devices].reshape(-1)
    attn_gain = gains[0]
    mlp_gain = gains[1]
    query_gain = spread_gain(gains[2], query_rank)
    latent_gain = spread_gain(gains[3], KVR)

    first_inverse = inverse
    first_low = low(flat_inputs.astype(jnp.float32) * first_inverse * attn_gain)
    latent_raw = matmul_plain(first_low, full_small)
    latent_mixed, latent_plain, latent_inverse = rms_scale(latent_raw[:, :KVR], latent_gain)
    both_cos = jnp.tile(local_cos, (batches, 1))
    both_sin = jnp.tile(local_sin, (batches, 1))
    key_rope_low = low(rope_apply(latent_raw[:, KVR:gain_place], both_cos, both_sin))
    near_own = jnp.concatenate([low(latent_mixed), key_rope_low], axis=1).reshape(
        batches, local_rows, gain_place
    )
    near_own, moved, wave, attn_out = hold((near_own, moved, wave, attn_out))
    near = lax.all_gather(near_own, "ctx", axis=1, tiled=True)
    crossed = [flip(held, 1) for held in (*wave, *moved)]
    out_half = attn_out.shape[0] // 2
    out_wave = [attn_out[:out_half], attn_out[out_half:]]
    out_moved = depart(out_wave, both_ways, 0)
    branch_grad = low(branch_scale * (cotangent[0].astype(jnp.float32) * live))
    crossed, wave, moved, branch_grad, bias, quad_cos, quad_ahead, quad_behind, query_gain = hold(
        (crossed, wave, moved, branch_grad, bias, quad_cos, quad_ahead, quad_behind, query_gain)
    )
    full_down, full_latent, full_query = place_shards(
        [
            [pieces_of(wave[i], moved[i], crossed[i], crossed[3 + i], ways[i])]
            for i in range(3)
        ]
    )
    query_mixed, query_plain, query_inverse = rms_scale(
        matmul_plain(first_low, full_down), query_gain
    )
    query_low = low(query_mixed)
    query_low, out_moved, out_wave, branch_grad, near, own_weights = hold(
        (query_low, out_moved, out_wave, branch_grad, near, (gate_weight, up_weight, down_weight))
    )
    latent_all = near[..., :KVR]
    key_rope_all = near[..., KVR:]
    quad_rope = jnp.tile(key_rope_all, (1, 1, QUAD))
    out_wave = join(out_wave, out_moved)
    for place in range(1, last):
        out_wave = join(out_wave, depart(out_wave, both_ways, place))
    out_moved = depart(out_wave, both_ways, last)
    other_weights = [flip(own_weights[0], 1)]
    in_halves = lambda values, batch: [values[batch, :half_rows], values[batch, half_rows:]]
    grad_wave = [in_halves(branch_grad, batch) for batch in range(batches)]
    grad_moved = [None] * batches
    grad_moved[0] = depart(grad_wave[0], both_ways, 0)
    query_turned, mixed, log_total = attend_forward(
        query_low.reshape(batches, local_rows, query_rank),
        latent_all,
        quad_rope,
        bias,
        quad_cos,
        quad_ahead,
        quad_behind,
        full_query,
        full_latent,
        quads,
    )
    out_moved, out_wave, mixed, grad_moved[0], grad_wave, other_weights, own_weights = hold(
        (out_moved, out_wave, mixed, grad_moved[0], grad_wave, other_weights, own_weights)
    )

    def onward(wave, moved):
        wave = join(wave, moved)
        for place in range(1, last):
            wave = join(wave, depart(wave, both_ways, place))
        return wave, depart(wave, both_ways, last)

    out_crossed = [flip(held, 1) for held in (*out_wave, *out_moved)]
    out_wave, out_moved, out_crossed, grad_wave, grad_moved[0], other_weights, own_weights = hold(
        (out_wave, out_moved, out_crossed, grad_wave, grad_moved[0], other_weights, own_weights)
    )
    grad_wave[0], grad_moved[0] = onward(grad_wave[0], grad_moved[0])
    other_weights += [flip(weight, 1) for weight in own_weights[1:]]
    (full_out,) = place_shards(
        [
            [
                pieces_of(out_wave[i], out_moved[i], out_crossed[i], out_crossed[2 + i], both_ways[i])
                for i in range(2)
            ]
        ]
    )
    mixed_flat = mixed.reshape(rows, H * DV)
    resid = flat_inputs.astype(jnp.float32) + branch_scale * matmul_plain(mixed_flat, full_out)
    second_normed, _, second_inverse = rms_scale(resid, mlp_gain)
    second_low = low(second_normed).reshape(batches, local_rows, width)
    of_batch = lambda values, batch: values[batch * local_rows : (batch + 1) * local_rows]
    second_low, grad_wave, grad_moved[0], other_weights, own_weights = hold(
        (second_low, grad_wave, grad_moved[0], other_weights, own_weights)
    )

    parts_of = lambda wave, moved: [wave[0], moved[0], wave[1], moved[1]]
    grad_parts = [parts_of(grad_wave[0], grad_moved[0])]
    rows_wave = [in_halves(second_low, batch) for batch in range(batches)]
    rows_moved = [depart(rows_wave[0], both_ways, 0), None]
    gate_all = jnp.concatenate([own_weights[0], other_weights[0]])
    rows_moved[0], rows_wave[0], gate_all = hold((rows_moved[0], rows_wave[0], gate_all))
    rows_wave[0], rows_moved[0] = onward(rows_wave[0], rows_moved[0])
    up_all = jnp.concatenate([own_weights[1], other_weights[1]])
    down_all = jnp.concatenate([own_weights[2], other_weights[2]])
    rows_moved[0], rows_wave, grad_wave[1], grad_parts, up_all, down_all = hold(
        (rows_moved[0], rows_wave, grad_wave[1], grad_parts, up_all, down_all)
    )

    quarter = sum(part.shape[0] for part in grad_parts[0]) // 4
    slots = tuple((place * quarter,) for place in range(4))
    rows_parts = [parts_of(rows_wave[0], rows_moved[0])]
    grad_moved[1] = depart(grad_wave[1], both_ways, 0)
    rows_moved[1] = depart(rows_wave[1], both_ways, 0)
    units = [feed_up(rows_parts[0], grad_parts[0], gate_all, up_all, down_all)]
    units, rows_moved[1], rows_wave[1], grad_wave[1], grad_moved[1] = hold(
        (units, rows_moved[1], rows_wave[1], grad_wave[1], grad_moved[1])
    )
    rows_wave[1], rows_moved[1] = onward(rows_wave[1], rows_moved[1])
    grad_wave[1], grad_moved[1] = onward(grad_wave[1], grad_moved[1])
    branch_parts = feed_down([units[0][0]], [down_all], slots)
    rows_grads = feed_down([units[0][1], units[0][2]], [gate_all, up_all], slots)
    rows_grads, branch_parts, units, rows_moved[1], rows_wave[1], grad_wave[1], grad_moved[1] = hold(
        (rows_grads, branch_parts, units, rows_moved[1], rows_wave[1], grad_wave[1], grad_moved[1])
    )

    def scatter_first(parts):
        return [parts[0], parts[2]], [flip(parts[1], bits[-1]), flip(parts[3], bits[0])]

    def scatter_next(kept, got, place):
        joined = [low(add_up(held, value)) for held, value in zip(kept, got)]
        half = joined[0].shape[0] // 2
        moved = [
            flip(joined[0][half:], bits[-1 - place]),
            flip(joined[1][half:], bits[place]),
        ]
        return [held[:half] for held in joined], moved

    def scatter_mid(kept, got):
        for place in range(1, last):
            kept, got = scatter_next(kept, got, place)
        return scatter_next(kept, got, last)

    def scatter_end(kept, got):
        return jnp.concatenate([add_up(held, value) for held, value in zip(kept, got)])

    out_ways = [scatter_first(branch_parts)]
    grad_ways = [scatter_first(rows_grads)]
    rows_parts.append(parts_of(rows_wave[1], rows_moved[1]))
    grad_parts.append(parts_of(grad_wave[1], grad_moved[1]))
    units.append(feed_up(rows_parts[1], grad_parts[1], gate_all, up_all, down_all))
    units, out_ways[0], rows_parts, grad_parts = hold((units, out_ways[0], rows_parts, grad_parts))

    out_ways[0] = scatter_mid(*out_ways[0])
    jobs = [
        ([of[0] for of in units], grad_parts),
        ([of[1] for of in units], rows_parts),
        ([of[2] for of in units], rows_parts),
    ]
    away = [weight_sums(lefts, rights, 1, None) for lefts, rights in jobs]
    away, grad_ways[0], out_ways[0], units = hold((away, grad_ways[0], out_ways[0], units))
    grad_ways[0] = scatter_mid(*grad_ways[0])
    back = [[flip(part, 1) for part in parts] for parts in away]
    branch_parts = feed_down([units[1][0]], [down_all], slots)
    back[0], branch_parts, out_ways[0] = hold((back[0], branch_parts, out_ways[0]))
    out_ways.append(scatter_first(branch_parts))
    own = [weight_sums(*jobs[0], 0, back[0])]
    line = LineSum()
    line.add(*own[0])
    sends, units, grad_ways[0], out_ways[0] = hold(
        (line.sends(), units, grad_ways[0], out_ways[0])
    )

    got = line.move(sends)
    own += [weight_sums(*jobs[i], 0, back[i]) for i in range(1, 3)]
    rows_grads = feed_down([units[1][1], units[1][2]], [gate_all, up_all], slots)
    got, own, rows_grads, out_ways[1] = hold((got, own, rows_grads, out_ways[1]))
    line.absorb(got)
    line.add(*own[1], *own[2])

    def collect(part):
        return lax.psum_scatter(part, "ctx", scatter_dimension=0, tiled=True).astype(jnp.float32)

    def grads_begin(batch, second_grad):
        second_plain = of_batch(resid, batch) * of_batch(second_inverse, batch)
        second_back, mlp_gain_grad = rms_back(
            second_grad, second_plain, of_batch(second_inverse, batch), mlp_gain
        )
        resid_grad = cotangent[0, batch].astype(jnp.float32) * live[batch] + second_back
        attn_grad = low(branch_scale * resid_grad)
        mixed_grad = low(matmul_right(attn_grad, full_out))
        return resid_grad, attn_grad, mixed_grad, mlp_gain_grad

    def grads_attend(batch, mixed_grad):
        query_raw_grad, key_up_part, value_up_part, latent_grad_all, rope_grad_all = attend_backward(
            query_turned[batch],
            mixed_grad,
            latent_all[batch],
            latent_all[batch].T,
            quad_rope[batch],
            key_rope_all[batch].T,
            bias[batch],
            log_total[batch],
            local_cos[:, :half].T,
            local_sin[:, :half].T,
            full_latent,
            quads,
        )
        key_rope_grad = rope_grad_all.reshape(seq_rows, QUAD, DR).sum(axis=1)
        latent_part = low(jnp.concatenate([latent_grad_all, key_rope_grad], axis=1))
        return query_raw_grad, key_up_part, value_up_part, latent_part

    def query_end(batch, query_raw_grad):
        query_mixed_grad = matmul_right(query_raw_grad, full_query)
        query_back, query_gain_grad = rms_back(
            query_mixed_grad, of_batch(query_plain, batch), of_batch(query_inverse, batch), query_gain
        )
        return low(query_back), query_gain_grad

    def grads_end(batch, query_back, collected, resid_grad):
        latent_back, latent_gain_grad = rms_back(
            collected[:, :KVR], of_batch(latent_plain, batch), of_batch(latent_inverse, batch), latent_gain
        )
        latent_raw_grad = pad_columns(
            low(
                jnp.concatenate(
                    [latent_back, rope_back(collected[:, KVR:], local_cos, local_sin)], axis=-1
                )
            ),
            full_small.shape[1],
        )
        first_grad = matmul_right(query_back, full_down) + matmul_right(latent_raw_grad, full_small)
        first_plain = of_batch(flat_inputs, batch).astype(jnp.float32) * of_batch(first_inverse, batch)
        first_back, attn_gain_grad = rms_back(
            first_grad, first_plain, of_batch(first_inverse, batch), attn_gain
        )
        return low(resid_grad + first_back), latent_raw_grad, attn_gain_grad, latent_gain_grad

    sends, rows_grads, grad_ways[0], out_ways[1] = hold(
        (line.sends(), rows_grads, grad_ways[0], out_ways[1])
    )
    got = line.move(sends)
    grad_ways.append(scatter_first(rows_grads))
    out_ways[1] = scatter_mid(*out_ways[1])
    begun = [grads_begin(0, scatter_end(*grad_ways[0]))]
    outputs = [low(of_batch(resid, 0) + branch_scale * scatter_end(*out_ways[0]))]
    got, begun, grad_ways[1], outputs = hold((got, begun, grad_ways[1], outputs))
    line.absorb(got)

    sends, grad_ways[1], begun = hold((line.sends(), grad_ways[1], begun))
    got = line.move(sends)
    grad_ways[1] = scatter_mid(*grad_ways[1])
    attended = [grads_attend(0, begun[0][2])]
    got, attended, grad_ways[1], begun = hold((got, attended, grad_ways[1], begun))
    line.absorb(got)

    sends, grad_ways[1], out_ways[1], attended = hold(
        (line.sends(), grad_ways[1], out_ways[1], attended)
    )
    got = line.move(sends)
    begun.append(grads_begin(1, scatter_end(*grad_ways[1])))
    outputs.append(low(of_batch(resid, 1) + branch_scale * scatter_end(*out_ways[1])))
    out_sum = low(matmul_left(mixed_flat, jnp.concatenate([begun[0][1], begun[1][1]])))
    got, begun, out_sum, outputs = hold((got, begun, out_sum, outputs))
    line.absorb(got)
    in_shards = lambda values: values.reshape(devices, -1, values.shape[-1])
    back_way = [1] + bits[::-1]
    back_other = [1] + bits
    out_sum = in_shards(out_sum)
    out_steps = [
        ScatterWhole(out_sum[:, :out_half], back_way),
        ScatterWhole(out_sum[:, out_half:], back_other),
    ]

    sends, begun, out_sends, attended = hold(
        (line.sends(), begun, [job.send() for job in out_steps], attended)
    )
    got = line.move(sends)
    out_got = [job.move(value) for job, value in zip(out_steps, out_sends)]
    collected = [collect(attended[0][3])]
    attended.append(grads_attend(1, begun[1][2]))
    got, attended, out_got, begun = hold((got, attended, out_got, begun))
    line.absorb(got)
    for job, value in zip(out_steps, out_got):
        job.absorb(value)

    sends, attended, out_sends = hold(
        (line.sends(), attended, [job.send() for job in out_steps])
    )
    got = line.move(sends)
    collected.append(collect(attended[1][3]))
    out_got = [job.move(value) for job, value in zip(out_steps, out_sends)]
    latent_up_sum = low(
        jnp.concatenate([attended[0][1] + attended[1][1], attended[0][2] + attended[1][2]], axis=1)
    )
    query_sum = low(matmul_left(query_low, jnp.concatenate([attended[0][0], attended[1][0]])))
    query_ends = [query_end(batch, attended[batch][0]) for batch in range(batches)]
    down_sum = low(matmul_left(first_low, jnp.concatenate([query_ends[0][0], query_ends[1][0]])))
    got, out_got, latent_up_sum, query_sum, down_sum, query_ends = hold(
        (got, out_got, latent_up_sum, query_sum, down_sum, query_ends)
    )
    line.absorb(got)
    for job, value in zip(out_steps, out_got):
        job.absorb(value)
    steps = [
        ScatterWhole(in_shards(query_sum), back_other),
        ScatterWhole(in_shards(latent_up_sum), back_way),
        ScatterWhole(in_shards(down_sum), back_way),
    ]

    small_steps = None
    while line.busy() or steps or small_steps != []:
        running = [job for job in out_steps + steps + (small_steps or []) if job.order]
        sends, values, query_ends, collected = hold(
            (line.sends(), [job.send() for job in running], query_ends, collected)
        )
        got = line.move(sends)
        values = [job.move(value) for job, value in zip(running, values)]
        if small_steps is None:
            ended = [
                grads_end(batch, query_ends[batch][0], collected[batch], begun[batch][0])
                for batch in range(batches)
            ]
            input_grads = [of[0] for of in ended]
            small_sum = matmul_left(first_low, jnp.concatenate([of[1] for of in ended]))
            places = lax.broadcasted_iota(jnp.int32, full_small.shape, 1) - gain_place
            gathered_gain = lambda gain: jnp.pad(
                gain.reshape(devices, -1), ((0, 0), (0, shard_rows - gain.shape[0] // devices))
            ).reshape(-1)
            gain_columns = [
                ended[0][2] + ended[1][2],
                begun[0][3] + begun[1][3],
                gathered_gain(query_ends[0][1] + query_ends[1][1]),
                gathered_gain(ended[0][3] + ended[1][3]),
            ]
            for place, gain in enumerate(gain_columns):
                small_sum = jnp.where(places == place, gain[:, None], small_sum)
            small_sum = low(small_sum)
            got, values, small_sum = hold((got, values, small_sum))
            small_steps = [ScatterWhole(in_shards(small_sum), back_other)]
        else:
            got, values = hold((got, values))
        line.absorb(got)
        for job, value in zip(running, values):
            job.absorb(value)
        if out_steps and not any(job.order for job in out_steps):
            line.add(jnp.concatenate([job.held[0] for job in out_steps]))
            out_steps = []
        if steps and not any(job.order for job in steps):
            line.add(*[job.held[0] for job in steps])
            steps = []
        if small_steps and not small_steps[0].order:
            line.add(small_steps[0].held[0])
            small_steps = []
    totals = [total.astype(jnp.float32) for total in line.held]
    ffn_totals = [jnp.concatenate(totals[2 * i : 2 * i + 2]) for i in (1, 2, 0)]
    out_total, query_total, latent_total, down_total, small_total = totals[6:]
    by_quad = query_total.reshape(-1, quads, QUAD * (DN + DR))
    query_up_total = jnp.concatenate(
        [
            by_quad[..., : QUAD * DN].reshape(-1, quads, QUAD, DN),
            by_quad[..., QUAD * DN :].reshape(-1, quads, QUAD, DR),
        ],
        axis=-1,
    ).reshape(query_up.shape)
    latent_up_total = jnp.concatenate(
        [
            latent_total[:, : H * DN].reshape(-1, H, DN),
            latent_total[:, H * DN :].reshape(-1, H, DV),
        ],
        axis=-1,
    ).reshape(latent_up.shape)
    return (
        jnp.stack(outputs)[None],
        jnp.stack(input_grads)[None],
        small_total[:, gain_place],
        down_total,
        small_total[: query_norm.shape[0], gain_place + 2],
        query_up_total,
        small_total[:, :gain_place],
        small_total[: latent_norm.shape[0], gain_place + 3],
        latent_up_total,
        out_total,
        small_total[:, gain_place + 1],
        ffn_totals[0],
        ffn_totals[1],
        ffn_totals[2],
    )


def solution(mesh):
    placed = (
        P("fsdp", None, "ctx", None),
        P("fsdp", None, "ctx", None),
        P("fsdp", None),
        P(),
        P("fsdp"),
        P("fsdp", None),
        P("fsdp"),
        P("fsdp", None),
        P("fsdp", None),
        P("fsdp"),
        P("fsdp", None),
        P("fsdp", None),
        P("fsdp"),
        P("fsdp", None),
        P("fsdp", None),
        P("fsdp", None),
    )
    return jax.shard_map(
        body,
        mesh=mesh,
        in_specs=placed,
        out_specs=(
            P("fsdp", None, "ctx", None),
            P("fsdp", None, "ctx", None),
            P("fsdp"),
            P("fsdp", None),
            P("fsdp"),
            P("fsdp", None),
            P("fsdp", None),
            P("fsdp"),
            P("fsdp", None),
            P("fsdp", None),
            P("fsdp"),
            P("fsdp", None),
            P("fsdp", None),
            P("fsdp", None),
        ),
        check_vma=False,
    )
```

```python
import functools
import math

import jax
import jax.numpy as jnp
from jax import lax
from jax.experimental import pallas as pl
from jax.experimental.pallas import tpu as pltpu
from jax.sharding import PartitionSpec as P

H = 40
DN = 64
DR = 32
DV = 64
KVR = 256
QUAD = 4


branch_scale = 1.4 / math.sqrt(62.0)
norm_eps = 1e-05
rope_base = 10000.0
lowest_score = -1e30
score_scale = (DN + DR) ** -0.5
exp_scale = math.log2(math.e) * score_scale


def rms_scale(values, gain):
    inverse = lax.rsqrt(jnp.mean(values * values, axis=-1, keepdims=True) + norm_eps)
    plain = values * inverse
    return (plain * gain, plain, inverse)


def rms_back(grad_out, plain, inverse, gain):
    gain_grad = jnp.sum(grad_out * plain, axis=0)
    scaled = grad_out * gain
    values_grad = inverse * (scaled - plain * jnp.mean(scaled * plain, axis=-1, keepdims=True))
    return (values_grad, gain_grad)


def rope_tables(positions, width):
    half = width // 2
    freq = rope_base ** (-(jnp.arange(half, dtype=jnp.float32) * 2.0 / width))
    angle = positions.astype(jnp.float32)[:, None] * freq[None, :]
    return (
        jnp.concatenate([jnp.cos(angle), jnp.cos(angle)], axis=-1),
        jnp.concatenate([jnp.sin(angle), jnp.sin(angle)], axis=-1),
    )


def turn_half(values):
    half = values.shape[-1] // 2
    return jnp.concatenate([-values[..., half:], values[..., :half]], axis=-1)


def turn_back(values):
    half = values.shape[-1] // 2
    return jnp.concatenate([values[..., half:], -values[..., :half]], axis=-1)


def rope_apply(values, cosine, sine):
    return values * cosine + turn_half(values) * sine


def rope_back(grads, cosine, sine):
    return grads * cosine + turn_back(grads * sine)


def matmul_plain(left, right):
    return jnp.dot(left, right, preferred_element_type=jnp.float32)


def matmul_left(left, right):
    return lax.dot_general(
        left, right, (((0,), (0,)), ((), ())), preferred_element_type=jnp.float32
    )


def matmul_right(left, right):
    return lax.dot_general(
        left, right, (((1,), (1,)), ((), ())), preferred_element_type=jnp.float32
    )


def flip(values, bit):
    count = lax.axis_size("fsdp")
    return lax.ppermute(values, "fsdp", [(i, i ^ bit) for i in range(count)])


def chip_bits():
    return [1 << k for k in range(1, lax.axis_size("fsdp").bit_length() - 1)]


def low(values):
    return values.astype(jnp.bfloat16)


def add_up(left, right):
    return left.astype(jnp.float32) + right.astype(jnp.float32)


def place_kernel(plan, me_ref, *refs):
    sources, outs, sems = refs[: len(plan)], refs[len(plan) : -1], refs[-1]
    me = me_ref[0]
    copies = []
    for source, (out, rows, places, stride, offset) in zip(sources, plan):
        for k, place in enumerate(places):
            start = pl.multiple_of((me ^ place) * stride + offset, 16)
            copies.append(
                pltpu.make_async_copy(
                    source.at[pl.ds(k * rows, rows)],
                    outs[out].at[pl.ds(start, rows)],
                    sems.at[len(copies)],
                )
            )
    for copy in copies:
        copy.start()
    for copy in copies:
        copy.wait()


def place_shards(groups):
    count = lax.axis_size("fsdp")
    me = lax.axis_index("fsdp").astype(jnp.int32).reshape(1)
    plan, sources, shapes = [], [], []
    for out, parts in enumerate(groups):
        heights = [sum(piece.shape[0] for piece, _ in part) // count for part in parts]
        offset = 0
        for part, rows in zip(parts, heights):
            for piece, places in part:
                plan.append((out, rows, tuple(places), sum(heights), offset))
                sources.append(piece)
            offset += rows
        shapes.append(jax.ShapeDtypeStruct((count * sum(heights), parts[0][0][0].shape[1]), jnp.bfloat16))
    anywhere = pl.BlockSpec(memory_space=pl.ANY)
    return pl.pallas_call(
        functools.partial(place_kernel, tuple(plan)),
        in_specs=[pl.BlockSpec(memory_space=pltpu.SMEM)] + [anywhere] * len(sources),
        out_specs=[pl.BlockSpec(memory_space=pltpu.VMEM)] * len(shapes),
        out_shape=shapes,
        scratch_shapes=[pltpu.SemaphoreType.DMA((sum(len(of[2]) for of in plan),))],
        compiler_params=pltpu.CompilerParams(vmem_limit_bytes=32 * 2**20),
        name="place_shards",
    )(me, *sources)


class ScatterWhole:
    def __init__(self, held, order):
        self.held = held
        self.order = list(order)
        self.left = [1 << k for k in range(held.shape[0].bit_length() - 2, -1, -1)]
        self.me = lax.axis_index("fsdp")

    def send(self):
        rows, width = self.held.shape[1:]
        place = self.left.index(self.order[0])
        below = 1 << (len(self.left) - place - 1)
        held = self.held.reshape(-1, 2, below, rows, width)
        mine = (self.me // self.order[0]) % 2
        self.kept = lax.dynamic_index_in_dim(held, mine, 1, keepdims=False)
        return lax.dynamic_index_in_dim(held, 1 - mine, 1, keepdims=False)

    def move(self, value):
        return flip(value, self.order[0])

    def absorb(self, value):
        self.held = low(add_up(self.kept, value)).reshape((-1,) + self.held.shape[1:])
        self.left.remove(self.order.pop(0))


def lane_part(values, width, place):
    lane = lax.broadcasted_iota(jnp.int32, values.shape, 1)
    return jnp.where(lane // width == place, values, 0.0)


def pair_rows(nope, rope, pair):
    both = nope[:, pair * 2 * DN : (pair + 1) * 2 * DN]
    return low(
        jnp.concatenate(
            [
                jnp.concatenate(
                    [lane_part(both, DN, head), lane_part(rope, DR, 2 * pair + head)], axis=1
                )
                for head in range(2)
            ],
            axis=0,
        )
    )


def forward_kernel(
    low_ref, latent_ref, rope_ref, bias_ref, cos_ref, ahead_ref, behind_ref,
    query_w, key_w, value_w, query_ref, mixed_ref, total_ref,
):
    rows = low_ref.shape[1]
    raw = matmul_plain(low_ref[0], query_w[...])
    nope = raw[:, : QUAD * DN]
    rope = raw[:, QUAD * DN :]
    lanes = QUAD * DR
    rope = (
        rope * cos_ref[...]
        + pltpu.roll(rope, lanes - DR // 2, 1) * ahead_ref[...]
        + pltpu.roll(rope, DR // 2, 1) * behind_ref[...]
    )
    query_ref[0] = low(jnp.concatenate([nope, rope], axis=1))
    latent = latent_ref[0]
    keys = low(matmul_plain(latent, key_w[...]))
    values = low(matmul_plain(latent, value_w[...])).T
    mixed = []
    for pair in range(2):
        key_cat = jnp.concatenate(
            [keys[:, pair * 2 * DN : (pair + 1) * 2 * DN], rope_ref[0]], axis=1
        )
        scores = matmul_right(key_cat, pair_rows(nope, rope, pair))
        for head in range(2):
            place = 2 * pair + head
            own = scores[:, head * rows : (head + 1) * rows] * exp_scale + bias_ref[0]
            top = jnp.max(own, axis=0, keepdims=True)
            expo = jnp.exp2(own - top)
            total = jnp.sum(expo, axis=0, keepdims=True)
            out = matmul_plain(values[place * DV : (place + 1) * DV], low(expo))
            mixed.append(out / total)
            total_ref[0, 0, place : place + 1, :] = top + jnp.log2(total)
    mixed_ref[0] = low(jnp.concatenate(mixed, axis=0).T)


def attend_forward(query_low, latent, rope_keys, bias, cosine, ahead, behind, query_w, latent_w, quads):
    batches, rows, rank = query_low.shape
    keys, width = latent.shape[1:]
    qw, kw, rw = QUAD * (DN + DR), QUAD * DN, QUAD * DR
    fixed = lambda b, j: (0, 0)
    whole = lambda b, j: (b, 0, 0)
    flops = batches * quads * (2 * keys * width * 2 * kw + 2 * rows * rank * qw + 4 * 4 * keys * rows * 256)
    return pl.pallas_call(
        forward_kernel,
        grid=(batches, quads),
        in_specs=[
            pl.BlockSpec((1, rows, rank), whole),
            pl.BlockSpec((1, keys, width), whole),
            pl.BlockSpec((1, keys, rw), whole),
            pl.BlockSpec((1, keys, rows), whole),
            pl.BlockSpec((rows, rw), fixed),
            pl.BlockSpec((rows, rw), fixed),
            pl.BlockSpec((rows, rw), fixed),
            pl.BlockSpec((rank, qw), lambda b, j: (0, j)),
            pl.BlockSpec((width, kw), lambda b, j: (0, j)),
            pl.BlockSpec((width, kw), lambda b, j: (0, quads + j)),
        ],
        out_specs=[
            pl.BlockSpec((1, rows, qw), lambda b, j: (b, 0, j)),
            pl.BlockSpec((1, rows, kw), lambda b, j: (b, 0, j)),
            pl.BlockSpec((1, 1, QUAD, rows), lambda b, j: (b, j, 0, 0)),
        ],
        out_shape=[
            jax.ShapeDtypeStruct((batches, rows, quads * qw), jnp.bfloat16),
            jax.ShapeDtypeStruct((batches, rows, quads * kw), jnp.bfloat16),
            jax.ShapeDtypeStruct((batches, quads, QUAD, rows), jnp.float32),
        ],
        compiler_params=pltpu.CompilerParams(
            dimension_semantics=("arbitrary", "arbitrary"), vmem_limit_bytes=48 * 2**20
        ),
        cost_estimate=pl.CostEstimate(
            flops=int(flops), bytes_accessed=40 * 2**20, transcendentals=batches * quads * 4 * keys * rows
        ),
        name="attend_forward",
    )(query_low, latent, rope_keys, bias, cosine, ahead, behind, query_w, latent_w, latent_w)


def backward_kernel(
    query_ref, grad_ref, latent_ref, flat_ref, rope_ref, turned_ref, bias_ref, total_ref,
    cos_ref, sin_ref, key_w, value_w,
    query_out, key_up_out, value_up_out, latent_out, rope_out,
):
    rows = query_ref.shape[0]
    half = DR // 2

    @pl.when(pl.program_id(0) == 0)
    def _():
        latent_out[...] = jnp.zeros_like(latent_out)
        rope_out[...] = jnp.zeros_like(rope_out)

    latent = latent_ref[...]
    keys = low(matmul_plain(latent, key_w[...]))
    values = low(matmul_plain(latent, value_w[...]))
    turned_keys = keys.T
    query = query_ref[...].astype(jnp.float32)
    nope = query[:, : QUAD * DN]
    rope = query[:, QUAD * DN :]
    grad = grad_ref[...].astype(jnp.float32)
    key_grads, value_grads, nope_grads, rope_grads = [], [], [], []
    for pair in range(2):
        lanes = slice(pair * 2 * DN, (pair + 1) * 2 * DN)
        key_cat = jnp.concatenate([keys[:, lanes], rope_ref[...]], axis=1)
        query_cat = pair_rows(nope, rope, pair)
        grad_cat = low(
            jnp.concatenate([lane_part(grad[:, lanes], DV, head) for head in range(2)], axis=0)
        )
        scores = matmul_right(key_cat, query_cat)
        prob_grads = matmul_right(values[:, lanes], grad_cat)
        probs_low, score_low = [], []
        for head in range(2):
            place = 2 * pair + head
            cut = slice(head * rows, (head + 1) * rows)
            probs = jnp.exp2(
                scores[:, cut] * exp_scale + bias_ref[...] - total_ref[0, place : place + 1, :]
            )
            mixed = probs * prob_grads[:, cut]
            dots = jnp.sum(mixed, axis=0, keepdims=True)
            score_grad = low(mixed - probs * dots)
            probs_low.append(low(probs))
            score_low.append(score_grad)
            left = jnp.concatenate(
                [turned_keys[place * DN : (place + 1) * DN], turned_ref[...]], axis=0
            )
            turned = matmul_plain(left, score_grad) * score_scale
            nope_grads.append(turned[:DN])
            upper, lower = turned[DN : DN + half], turned[DN + half :]
            rope_grads.append(upper * cos_ref[...] + lower * sin_ref[...])
            rope_grads.append(lower * cos_ref[...] - upper * sin_ref[...])
        value_grads.append(matmul_plain(jnp.concatenate(probs_low, axis=1), grad_cat))
        key_cat_grad = matmul_plain(jnp.concatenate(score_low, axis=1), query_cat)
        key_grads.append(key_cat_grad[:, : 2 * DN])
        rope_out[...] += key_cat_grad[:, 2 * DN :] * score_scale
    query_out[...] = low(jnp.concatenate(nope_grads + rope_grads, axis=0).T)
    key_grad = low(jnp.concatenate(key_grads, axis=1) * score_scale)
    value_grad = low(jnp.concatenate(value_grads, axis=1))
    key_up_out[...] = matmul_plain(flat_ref[...], key_grad)
    value_up_out[...] = matmul_plain(flat_ref[...], value_grad)
    latent_out[...] += matmul_right(key_grad, key_w[...]) + matmul_right(value_grad, value_w[...])


def attend_backward(query, grad, latent, latent_flat, rope_keys, rope_flat, bias, totals, cos_flat, sin_flat, latent_w, quads):
    rows = query.shape[0]
    keys, width = latent.shape
    qw, kw, rw = QUAD * (DN + DR), QUAD * DN, QUAD * DR
    fixed = lambda j: (0, 0)
    step = lambda j: (0, j)
    flops = quads * (2 * keys * width * 6 * kw + 5 * 4 * 2 * keys * rows * 256)
    return pl.pallas_call(
        backward_kernel,
        grid=(quads,),
        in_specs=[
            pl.BlockSpec((rows, qw), step),
            pl.BlockSpec((rows, kw), step),
            pl.BlockSpec((keys, width), fixed),
            pl.BlockSpec((width, keys), fixed),
            pl.BlockSpec((keys, rw), fixed),
            pl.BlockSpec((DR, keys), fixed),
            pl.BlockSpec((keys, rows), fixed),
            pl.BlockSpec((1, QUAD, rows), lambda j: (j, 0, 0)),
            pl.BlockSpec((DR // 2, rows), fixed),
            pl.BlockSpec((DR // 2, rows), fixed),
            pl.BlockSpec((width, kw), step),
            pl.BlockSpec((width, kw), lambda j: (0, quads + j)),
        ],
        out_specs=[
            pl.BlockSpec((rows, qw), step),
            pl.BlockSpec((width, kw), step),
            pl.BlockSpec((width, kw), step),
            pl.BlockSpec((keys, width), fixed),
            pl.BlockSpec((keys, rw), fixed),
        ],
        out_shape=[
            jax.ShapeDtypeStruct((rows, quads * qw), jnp.bfloat16),
            jax.ShapeDtypeStruct((width, quads * kw), jnp.float32),
            jax.ShapeDtypeStruct((width, quads * kw), jnp.float32),
            jax.ShapeDtypeStruct((keys, width), jnp.float32),
            jax.ShapeDtypeStruct((keys, rw), jnp.float32),
        ],
        compiler_params=pltpu.CompilerParams(
            dimension_semantics=("arbitrary",), vmem_limit_bytes=48 * 2**20
        ),
        cost_estimate=pl.CostEstimate(
            flops=int(flops), bytes_accessed=25 * 2**20, transcendentals=quads * 4 * keys * rows
        ),
        name="attend_backward",
    )(query, grad, latent, latent_flat, rope_keys, rope_flat, bias, totals, cos_flat, sin_flat, latent_w, latent_w)


class LineSum:
    def __init__(self):
        self.count = lax.axis_size("ctx")
        self.me = lax.axis_index("ctx")
        self.hops = self.count // 2 - 1
        self.held = []
        self.stage = []
        self.queue = []

    def add(self, *pieces):
        for piece in pieces:
            self.queue.append(len(self.held))
            self.held.append(piece)
            self.stage.append(None)

    def busy(self):
        return bool(self.queue) or any(s is not None and s >= 0 for s in self.stage)

    def outer(self, hop):
        return (self.me == hop) | (self.me == self.count - 1 - hop)

    def sends(self):
        if self.queue:
            self.stage[self.queue.pop(0)] = 0
        self.plan, values = [], []
        at = {stage: item for item, stage in enumerate(self.stage) if stage is not None}
        last = self.count - 1
        for hop in range(self.hops):
            entering, leaving = at.get(hop), at.get(2 * self.hops - hop)
            inward = [(hop, hop + 1), (last - hop, last - hop - 1)]
            outward = [(to, source) for source, to in inward]
            both = entering is not None and leaving is not None
            if both and self.held[entering].shape == self.held[leaving].shape:
                self.plan.append((hop, entering, leaving, inward + outward))
                values.append(
                    jnp.where(self.outer(hop), self.held[entering], self.held[leaving])
                )
                continue
            if entering is not None:
                self.plan.append((hop, entering, None, inward))
                values.append(self.held[entering])
            if leaving is not None:
                self.plan.append((hop, None, leaving, outward))
                values.append(self.held[leaving])
        crossing = at.get(self.hops)
        if crossing is not None:
            self.plan.append(
                (None, crossing, None, [(self.hops, self.hops + 1), (self.hops + 1, self.hops)])
            )
            values.append(self.held[crossing])
        return values

    def move(self, values):
        return [lax.ppermute(value, "ctx", pairs) for value, (_, _, _, pairs) in zip(values, self.plan)]

    def absorb(self, values):
        for value, (hop, entering, leaving, _) in zip(values, self.plan):
            if entering is not None:
                self.held[entering] = low(add_up(self.held[entering], value))
            if leaving is not None:
                self.held[leaving] = jnp.where(self.outer(hop), value, self.held[leaving])
        for item, stage in enumerate(self.stage):
            if stage is not None:
                self.stage[item] = stage + 1 if stage < 2 * self.hops else None


def up_kernel(parts, gate_w, up_w, down_w, *refs):
    rows_refs, grad_refs = refs[:parts], refs[parts : 2 * parts]
    hidden_ref, gate_ref, up_ref = refs[2 * parts :]
    start = 0
    for rows_ref, grad_ref in zip(rows_refs, grad_refs):
        cut = slice(start, start + rows_ref.shape[0])
        start += rows_ref.shape[0]
        gate_value = matmul_right(gate_w[...], rows_ref[...])
        up_value = matmul_right(up_w[...], rows_ref[...])
        hidden_grad = matmul_right(down_w[...], grad_ref[...])
        sigmoid_gate = 1.0 / (1.0 + jnp.exp(-gate_value))
        silu_gate = gate_value * sigmoid_gate
        hidden_ref[:, cut] = low(silu_gate * up_value)
        gate_ref[:, cut] = low(
            hidden_grad * up_value * sigmoid_gate * (1.0 + gate_value * (1.0 - sigmoid_gate))
        )
        up_ref[:, cut] = low(hidden_grad * silu_gate)


def hidden_tile(units):
    return max(size for size in range(16, 401, 16) if units % size == 0)


def feed_up(rows_parts, grad_parts, gate_all, up_all, down_all):
    units, width = gate_all.shape
    tile = hidden_tile(units)
    rows = sum(part.shape[0] for part in rows_parts)
    whole = [
        pl.BlockSpec(part.shape, lambda i: (0, 0), pipeline_mode=pl.Buffered(1))
        for part in (*rows_parts, *grad_parts)
    ]
    return pl.pallas_call(
        functools.partial(up_kernel, len(rows_parts)),
        grid=(units // tile,),
        in_specs=[pl.BlockSpec((tile, width), lambda i: (i, 0))] * 3 + whole,
        out_specs=[pl.BlockSpec((tile, rows), lambda i: (i, 0))] * 3,
        out_shape=[jax.ShapeDtypeStruct((units, rows), jnp.bfloat16)] * 3,
        compiler_params=pltpu.CompilerParams(
            dimension_semantics=("arbitrary",), vmem_limit_bytes=52 * 2**20
        ),
        cost_estimate=pl.CostEstimate(
            flops=6 * units * width * rows,
            bytes_accessed=6 * units * width + 4 * rows * width + 6 * units * rows,
            transcendentals=units * rows,
        ),
        name="feed_up",
    )(gate_all, up_all, down_all, *rows_parts, *grad_parts)


def down_kernel(pairs, slots, *refs):
    units, weights = refs[:pairs], refs[pairs : 2 * pairs]
    outs, turned = refs[2 * pairs : -pairs], refs[-pairs:]

    @pl.when(pl.program_id(0) == 0)
    def _():
        for unit_ref, turned_ref in zip(units, turned):
            turned_ref[...] = unit_ref[...].T

    total = matmul_plain(turned[0][...], weights[0][...])
    for place in range(1, pairs):
        total += matmul_plain(turned[place][...], weights[place][...])
    for out, starts in zip(outs, slots):
        step = out.shape[0] // len(starts)
        for place, start in enumerate(starts):
            out[place * step : (place + 1) * step] = low(total[start : start + step])


def feed_down(units, weights, slots):
    parts = len(slots)
    depth, rows = units[0].shape
    width = weights[0].shape[1]
    tile = 512 if width % 512 == 0 else width
    return pl.pallas_call(
        functools.partial(down_kernel, len(units), slots),
        grid=(width // tile,),
        in_specs=[pl.BlockSpec((depth, rows), lambda j: (0, 0), pipeline_mode=pl.Buffered(1))]
        * len(units)
        + [pl.BlockSpec((depth, tile), lambda j: (0, j))] * len(units),
        out_specs=[pl.BlockSpec((rows // parts, tile), lambda j: (0, j))] * parts,
        out_shape=[jax.ShapeDtypeStruct((rows // parts, width), jnp.bfloat16)] * parts,
        scratch_shapes=[pltpu.VMEM((rows, depth), jnp.bfloat16)] * len(units),
        compiler_params=pltpu.CompilerParams(
            dimension_semantics=("arbitrary",), vmem_limit_bytes=48 * 2**20
        ),
        cost_estimate=pl.CostEstimate(
            flops=2 * len(units) * depth * rows * width,
            bytes_accessed=2 * len(units) * depth * (rows + width) + 2 * rows * width,
            transcendentals=0,
        ),
        name="feed_down",
    )(*units, *weights)


def weight_kernel(lefts, counts, fresh, *refs):
    left_refs, right_refs = refs[:lefts], refs[lefts : lefts + sum(counts)]
    half = left_refs[0].shape[0] // 2
    total, start = None, 0
    for left, count in zip(left_refs, counts):
        right = jnp.concatenate([ref[...] for ref in right_refs[start : start + count]], axis=0)
        start += count
        product = matmul_plain(left[...], right)
        total = product if total is None else total + product
    rest = refs[lefts + sum(counts) :]
    if fresh:
        upper, lower = rest
        upper[...] = low(total[:half])
        lower[...] = low(total[half:])
    else:
        upper_in, lower_in, upper, lower = rest
        upper[...] = low(total[:half] + upper_in[...].astype(jnp.float32))
        lower[...] = low(total[half:] + lower_in[...].astype(jnp.float32))


def weight_sums(lefts, rights, place, held):
    rows, depth = lefts[0].shape[0] // 2, lefts[0].shape[1]
    width = rights[0][0].shape[1]
    tile = 512 if width % 512 == 0 else width
    part = jax.ShapeDtypeStruct((rows // 2, width), jnp.bfloat16)
    part_spec = pl.BlockSpec((rows // 2, tile), lambda j: (0, j))
    flat = [piece for pieces in rights for piece in pieces]
    return pl.pallas_call(
        functools.partial(
            weight_kernel, len(lefts), tuple(len(pieces) for pieces in rights), held is None
        ),
        grid=(width // tile,),
        in_specs=[pl.BlockSpec((rows, depth), lambda j: (place, 0))] * len(lefts)
        + [pl.BlockSpec((piece.shape[0], tile), lambda j: (0, j)) for piece in flat]
        + ([] if held is None else [part_spec] * 2),
        out_specs=[part_spec] * 2,
        out_shape=[part] * 2,
        compiler_params=pltpu.CompilerParams(
            dimension_semantics=("arbitrary",), vmem_limit_bytes=40 * 2**20
        ),
        cost_estimate=pl.CostEstimate(
            flops=2 * len(lefts) * rows * depth * width,
            bytes_accessed=2 * len(lefts) * (rows * depth + depth * width) + 2 * rows * width,
            transcendentals=0,
        ),
        name="weight_sums",
    )(*lefts, *flat, *(held or ()))


def pad_columns(values, width):
    return jnp.pad(values, ((0, 0), (0, width - values.shape[1])))


def up_to(width):
    return (width + 127) // 128 * 128


def body(
    activations,
    cotangent,
    seq_length,
    block_order,
    attn_norm,
    query_down,
    query_norm,
    query_up,
    latent_down,
    latent_norm,
    latent_up,
    attn_out,
    mlp_norm,
    gate_weight,
    up_weight,
    down_weight,
):
    ctx_count = lax.axis_size("ctx")
    ctx_place = lax.axis_index("ctx")
    batches = activations.shape[1]
    local_rows = activations.shape[2]
    width = activations.shape[3]
    seq_rows = local_rows * ctx_count
    blocks = block_order.shape[0]
    block_size = seq_rows // blocks
    quads = query_up.shape[1] // (QUAD * (DN + DR))
    query_rank = query_down.shape[1]
    bits = chip_bits()

    every_row = jnp.arange(seq_rows, dtype=jnp.int32)
    block_of = every_row // block_size
    placed = jnp.sum(
        jnp.where(
            block_of[:, None] == jnp.arange(blocks, dtype=jnp.int32)[None, :],
            block_order[None, :],
            0,
        ),
        axis=1,
    )
    stored_pos = placed * block_size + every_row % block_size
    query_pos = lax.dynamic_slice_in_dim(stored_pos, ctx_place * local_rows, local_rows)
    key_pos = stored_pos
    local_cos, local_sin = rope_tables(query_pos, DR)
    half = DR // 2
    nothing = jnp.zeros_like(local_sin[:, :half])
    quad_cos = jnp.tile(local_cos, (1, QUAD))
    quad_ahead = jnp.tile(jnp.concatenate([-local_sin[:, :half], nothing], axis=1), (1, QUAD))
    quad_behind = jnp.tile(jnp.concatenate([nothing, local_sin[:, :half]], axis=1), (1, QUAD))
    lengths = seq_length[0]
    allowed = (key_pos[None, :, None] <= query_pos[None, None, :]) & (
        key_pos[None, :, None] < lengths[:, None, None]
    )
    bias = jnp.where(allowed, 0.0, lowest_score).astype(jnp.float32)

    hold = lax.optimization_barrier
    rows = batches * local_rows
    half_rows = local_rows // 2
    devices = lax.axis_size("fsdp")
    one_way = tuple(bits)
    other_way = tuple(bits[::-1])
    both_ways = (one_way, other_way)
    last = len(bits) - 1

    def depart(wave, ways, place):
        return [flip(held, way[place]) for held, way in zip(wave, ways)]

    def join(wave, moved):
        return [jnp.concatenate([held, got]) for held, got in zip(wave, moved)]

    shard_rows = query_down.shape[0]
    column = lambda gain: jnp.pad(gain[:, None], ((0, shard_rows - gain.shape[0]), (0, 0)))
    gain_place = KVR + DR
    small_shard = pad_columns(
        jnp.concatenate(
            [latent_down] + [column(gain) for gain in (attn_norm, mlp_norm, query_norm, latent_norm)],
            axis=1,
        ),
        up_to(gain_place + 4),
    )
    small_wave = [small_shard[: shard_rows // 2], small_shard[shard_rows // 2 :]]
    small_moved = depart(small_wave, both_ways, 0)
    by_quad = query_up.reshape(-1, quads, QUAD, DN + DR)
    query_shard = jnp.concatenate(
        [
            by_quad[..., :DN].reshape(-1, quads, QUAD * DN),
            by_quad[..., DN:].reshape(-1, quads, QUAD * DR),
        ],
        axis=2,
    ).reshape(query_up.shape)
    by_head = latent_up.reshape(-1, H, DN + DV)
    latent_shard = jnp.concatenate(
        [by_head[..., :DN].reshape(-1, H * DN), by_head[..., DN:].reshape(-1, H * DV)], axis=1
    )
    wave = [query_down, latent_shard, query_shard]
    ways = (one_way, one_way, other_way)
    moved = depart(wave, ways, 0)

    def places_of(way, bit):
        places = [0]
        for step in way[:-1]:
            places = places + [place ^ step for place in places]
        return [place ^ bit for place in places], [place ^ way[-1] ^ bit for place in places]

    def pieces_of(held, got, held_crossed, got_crossed, way):
        pieces = []
        for first, second, bit in ((held, got, 0), (held_crossed, got_crossed, 1)):
            for piece, places in zip((first, second), places_of(way, bit)):
                pieces.append((piece, places))
        return pieces

    small_moved, small_wave = hold((small_moved, small_wave))
    small_wave = join(small_wave, small_moved)
    for place in range(1, last):
        small_wave = join(small_wave, depart(small_wave, both_ways, place))
    small_moved = depart(small_wave, both_ways, last)
    lengths_live = query_pos[None, :] < lengths[:, None]
    live = lengths_live.astype(jnp.float32)[..., None]
    flat_inputs = activations[0].reshape(rows, width)
    inverse = lax.rsqrt(
        jnp.mean(flat_inputs.astype(jnp.float32) ** 2, axis=-1, keepdims=True) + norm_eps
    )
    small_moved, small_wave, inverse, moved, wave = hold(
        (small_moved, small_wave, inverse, moved, wave)
    )
    small_crossed = [flip(held, 1) for held in (*small_wave, *small_moved)]
    wave = join(wave, moved)
    for place in range(1, last):
        wave = join(wave, depart(wave, ways, place))
    small_crossed, small_wave, small_moved, wave = hold(
        (small_crossed, small_wave, small_moved, wave)
    )
    moved = depart(wave, ways, last)
    (full_small,) = place_shards(
        [
            [
                pieces_of(small_wave[i], small_moved[i], small_crossed[i], small_crossed[2 + i], both_ways[i])
                for i in range(2)
            ]
        ]
    )
    gains = full_small[:, gain_place : gain_place + 4].astype(jnp.float32).T
    spread_gain = lambda gain, size: gain.reshape(devices, -1)[:, : size // devices].reshape(-1)
    attn_gain = gains[0]
    mlp_gain = gains[1]
    query_gain = spread_gain(gains[2], query_rank)
    latent_gain = spread_gain(gains[3], KVR)

    first_inverse = inverse
    first_low = low(flat_inputs.astype(jnp.float32) * first_inverse * attn_gain)
    latent_raw = matmul_plain(first_low, full_small)
    latent_mixed, latent_plain, latent_inverse = rms_scale(latent_raw[:, :KVR], latent_gain)
    both_cos = jnp.tile(local_cos, (batches, 1))
    both_sin = jnp.tile(local_sin, (batches, 1))
    key_rope_low = low(rope_apply(latent_raw[:, KVR:gain_place], both_cos, both_sin))
    near_own = jnp.concatenate([low(latent_mixed), key_rope_low], axis=1).reshape(
        batches, local_rows, gain_place
    )
    near_own, moved, wave, attn_out = hold((near_own, moved, wave, attn_out))
    near = lax.all_gather(near_own, "ctx", axis=1, tiled=True)
    crossed = [flip(held, 1) for held in (*wave, *moved)]
    out_half = attn_out.shape[0] // 2
    out_wave = [attn_out[:out_half], attn_out[out_half:]]
    out_moved = depart(out_wave, both_ways, 0)
    branch_grad = low(branch_scale * (cotangent[0].astype(jnp.float32) * live))
    crossed, wave, moved, branch_grad, bias, quad_cos, quad_ahead, quad_behind, query_gain = hold(
        (crossed, wave, moved, branch_grad, bias, quad_cos, quad_ahead, quad_behind, query_gain)
    )
    full_down, full_latent, full_query = place_shards(
        [
            [pieces_of(wave[i], moved[i], crossed[i], crossed[3 + i], ways[i])]
            for i in range(3)
        ]
    )
    query_mixed, query_plain, query_inverse = rms_scale(
        matmul_plain(first_low, full_down), query_gain
    )
    query_low = low(query_mixed)
    query_low, out_moved, out_wave, branch_grad, near, own_weights = hold(
        (query_low, out_moved, out_wave, branch_grad, near, (gate_weight, up_weight, down_weight))
    )
    latent_all = near[..., :KVR]
    key_rope_all = near[..., KVR:]
    quad_rope = jnp.tile(key_rope_all, (1, 1, QUAD))
    out_wave = join(out_wave, out_moved)
    for place in range(1, last):
        out_wave = join(out_wave, depart(out_wave, both_ways, place))
    out_moved = depart(out_wave, both_ways, last)
    other_weights = [flip(own_weights[0], 1)]
    in_halves = lambda values, batch: [values[batch, :half_rows], values[batch, half_rows:]]
    grad_wave = [in_halves(branch_grad, batch) for batch in range(batches)]
    grad_moved = [None] * batches
    grad_moved[0] = depart(grad_wave[0], both_ways, 0)
    query_turned, mixed, log_total = attend_forward(
        query_low.reshape(batches, local_rows, query_rank),
        latent_all,
        quad_rope,
        bias,
        quad_cos,
        quad_ahead,
        quad_behind,
        full_query,
        full_latent,
        quads,
    )
    out_moved, out_wave, mixed, grad_moved[0], grad_wave, other_weights, own_weights = hold(
        (out_moved, out_wave, mixed, grad_moved[0], grad_wave, other_weights, own_weights)
    )

    def onward(wave, moved):
        wave = join(wave, moved)
        for place in range(1, last):
            wave = join(wave, depart(wave, both_ways, place))
        return wave, depart(wave, both_ways, last)

    out_crossed = [flip(held, 1) for held in (*out_wave, *out_moved)]
    out_wave, out_moved, out_crossed, grad_wave, grad_moved[0], other_weights, own_weights = hold(
        (out_wave, out_moved, out_crossed, grad_wave, grad_moved[0], other_weights, own_weights)
    )
    grad_wave[0], grad_moved[0] = onward(grad_wave[0], grad_moved[0])
    other_weights += [flip(weight, 1) for weight in own_weights[1:]]
    (full_out,) = place_shards(
        [
            [
                pieces_of(out_wave[i], out_moved[i], out_crossed[i], out_crossed[2 + i], both_ways[i])
                for i in range(2)
            ]
        ]
    )
    mixed_flat = mixed.reshape(rows, H * DV)
    resid = flat_inputs.astype(jnp.float32) + branch_scale * matmul_plain(mixed_flat, full_out)
    second_normed, _, second_inverse = rms_scale(resid, mlp_gain)
    second_low = low(second_normed).reshape(batches, local_rows, width)
    of_batch = lambda values, batch: values[batch * local_rows : (batch + 1) * local_rows]
    second_low, grad_wave, grad_moved[0], other_weights, own_weights = hold(
        (second_low, grad_wave, grad_moved[0], other_weights, own_weights)
    )

    parts_of = lambda wave, moved: [wave[0], moved[0], wave[1], moved[1]]
    grad_parts = [parts_of(grad_wave[0], grad_moved[0])]
    rows_wave = [in_halves(second_low, batch) for batch in range(batches)]
    rows_moved = [depart(rows_wave[0], both_ways, 0), None]
    gate_all = jnp.concatenate([own_weights[0], other_weights[0]])
    rows_moved[0], rows_wave[0], gate_all = hold((rows_moved[0], rows_wave[0], gate_all))
    rows_wave[0], rows_moved[0] = onward(rows_wave[0], rows_moved[0])
    up_all = jnp.concatenate([own_weights[1], other_weights[1]])
    down_all = jnp.concatenate([own_weights[2], other_weights[2]])
    rows_moved[0], rows_wave, grad_wave[1], grad_parts, up_all, down_all = hold(
        (rows_moved[0], rows_wave, grad_wave[1], grad_parts, up_all, down_all)
    )

    quarter = sum(part.shape[0] for part in grad_parts[0]) // 4
    slots = tuple((place * quarter,) for place in range(4))
    rows_parts = [parts_of(rows_wave[0], rows_moved[0])]
    grad_moved[1] = depart(grad_wave[1], both_ways, 0)
    rows_moved[1] = depart(rows_wave[1], both_ways, 0)
    units = [feed_up(rows_parts[0], grad_parts[0], gate_all, up_all, down_all)]
    units, rows_moved[1], rows_wave[1], grad_wave[1], grad_moved[1] = hold(
        (units, rows_moved[1], rows_wave[1], grad_wave[1], grad_moved[1])
    )
    rows_wave[1], rows_moved[1] = onward(rows_wave[1], rows_moved[1])
    grad_wave[1], grad_moved[1] = onward(grad_wave[1], grad_moved[1])
    branch_parts = feed_down([units[0][0]], [down_all], slots)
    rows_grads = feed_down([units[0][1], units[0][2]], [gate_all, up_all], slots)
    rows_grads, branch_parts, units, rows_moved[1], rows_wave[1], grad_wave[1], grad_moved[1] = hold(
        (rows_grads, branch_parts, units, rows_moved[1], rows_wave[1], grad_wave[1], grad_moved[1])
    )

    def scatter_first(parts):
        return [parts[0], parts[2]], [flip(parts[1], bits[-1]), flip(parts[3], bits[0])]

    def scatter_next(kept, got, place):
        joined = [low(add_up(held, value)) for held, value in zip(kept, got)]
        half = joined[0].shape[0] // 2
        moved = [
            flip(joined[0][half:], bits[-1 - place]),
            flip(joined[1][half:], bits[place]),
        ]
        return [held[:half] for held in joined], moved

    def scatter_mid(kept, got):
        for place in range(1, last):
            kept, got = scatter_next(kept, got, place)
        return scatter_next(kept, got, last)

    def scatter_end(kept, got):
        return jnp.concatenate([add_up(held, value) for held, value in zip(kept, got)])

    out_ways = [scatter_first(branch_parts)]
    grad_ways = [scatter_first(rows_grads)]
    rows_parts.append(parts_of(rows_wave[1], rows_moved[1]))
    grad_parts.append(parts_of(grad_wave[1], grad_moved[1]))
    units.append(feed_up(rows_parts[1], grad_parts[1], gate_all, up_all, down_all))
    units, out_ways[0], rows_parts, grad_parts = hold((units, out_ways[0], rows_parts, grad_parts))

    out_ways[0] = scatter_mid(*out_ways[0])
    jobs = [
        ([of[0] for of in units], grad_parts),
        ([of[1] for of in units], rows_parts),
        ([of[2] for of in units], rows_parts),
    ]
    away = [weight_sums(lefts, rights, 1, None) for lefts, rights in jobs]
    away, grad_ways[0], out_ways[0], units = hold((away, grad_ways[0], out_ways[0], units))
    grad_ways[0] = scatter_mid(*grad_ways[0])
    back = [[flip(part, 1) for part in parts] for parts in away]
    branch_parts = feed_down([units[1][0]], [down_all], slots)
    back[0], branch_parts, out_ways[0] = hold((back[0], branch_parts, out_ways[0]))
    out_ways.append(scatter_first(branch_parts))
    own = [weight_sums(*jobs[0], 0, back[0])]
    line = LineSum()
    line.add(*own[0])
    sends, units, grad_ways[0], out_ways[0] = hold(
        (line.sends(), units, grad_ways[0], out_ways[0])
    )

    got = line.move(sends)
    own += [weight_sums(*jobs[i], 0, back[i]) for i in range(1, 3)]
    rows_grads = feed_down([units[1][1], units[1][2]], [gate_all, up_all], slots)
    got, own, rows_grads, out_ways[1] = hold((got, own, rows_grads, out_ways[1]))
    line.absorb(got)
    line.add(*own[1], *own[2])

    def collect(part):
        return lax.psum_scatter(part, "ctx", scatter_dimension=0, tiled=True).astype(jnp.float32)

    def grads_begin(batch, second_grad):
        second_plain = of_batch(resid, batch) * of_batch(second_inverse, batch)
        second_back, mlp_gain_grad = rms_back(
            second_grad, second_plain, of_batch(second_inverse, batch), mlp_gain
        )
        resid_grad = cotangent[0, batch].astype(jnp.float32) * live[batch] + second_back
        attn_grad = low(branch_scale * resid_grad)
        mixed_grad = low(matmul_right(attn_grad, full_out))
        return resid_grad, attn_grad, mixed_grad, mlp_gain_grad

    def grads_attend(batch, mixed_grad):
        query_raw_grad, key_up_part, value_up_part, latent_grad_all, rope_grad_all = attend_backward(
            query_turned[batch],
            mixed_grad,
            latent_all[batch],
            latent_all[batch].T,
            quad_rope[batch],
            key_rope_all[batch].T,
            bias[batch],
            log_total[batch],
            local_cos[:, :half].T,
            local_sin[:, :half].T,
            full_latent,
            quads,
        )
        key_rope_grad = rope_grad_all.reshape(seq_rows, QUAD, DR).sum(axis=1)
        latent_part = low(jnp.concatenate([latent_grad_all, key_rope_grad], axis=1))
        return query_raw_grad, key_up_part, value_up_part, latent_part

    def query_end(batch, query_raw_grad):
        query_mixed_grad = matmul_right(query_raw_grad, full_query)
        query_back, query_gain_grad = rms_back(
            query_mixed_grad, of_batch(query_plain, batch), of_batch(query_inverse, batch), query_gain
        )
        return low(query_back), query_gain_grad

    def grads_end(batch, query_back, collected, resid_grad):
        latent_back, latent_gain_grad = rms_back(
            collected[:, :KVR], of_batch(latent_plain, batch), of_batch(latent_inverse, batch), latent_gain
        )
        latent_raw_grad = pad_columns(
            low(
                jnp.concatenate(
                    [latent_back, rope_back(collected[:, KVR:], local_cos, local_sin)], axis=-1
                )
            ),
            full_small.shape[1],
        )
        first_grad = matmul_right(query_back, full_down) + matmul_right(latent_raw_grad, full_small)
        first_plain = of_batch(flat_inputs, batch).astype(jnp.float32) * of_batch(first_inverse, batch)
        first_back, attn_gain_grad = rms_back(
            first_grad, first_plain, of_batch(first_inverse, batch), attn_gain
        )
        return low(resid_grad + first_back), latent_raw_grad, attn_gain_grad, latent_gain_grad

    sends, rows_grads, grad_ways[0], out_ways[1] = hold(
        (line.sends(), rows_grads, grad_ways[0], out_ways[1])
    )
    got = line.move(sends)
    grad_ways.append(scatter_first(rows_grads))
    out_ways[1] = scatter_mid(*out_ways[1])
    begun = [grads_begin(0, scatter_end(*grad_ways[0]))]
    outputs = [low(of_batch(resid, 0) + branch_scale * scatter_end(*out_ways[0]))]
    got, begun, grad_ways[1], outputs = hold((got, begun, grad_ways[1], outputs))
    line.absorb(got)

    sends, grad_ways[1], begun = hold((line.sends(), grad_ways[1], begun))
    got = line.move(sends)
    grad_ways[1] = scatter_mid(*grad_ways[1])
    attended = [grads_attend(0, begun[0][2])]
    got, attended, grad_ways[1], begun = hold((got, attended, grad_ways[1], begun))
    line.absorb(got)

    sends, grad_ways[1], out_ways[1], attended = hold(
        (line.sends(), grad_ways[1], out_ways[1], attended)
    )
    got = line.move(sends)
    begun.append(grads_begin(1, scatter_end(*grad_ways[1])))
    outputs.append(low(of_batch(resid, 1) + branch_scale * scatter_end(*out_ways[1])))
    out_sum = low(matmul_left(mixed_flat, jnp.concatenate([begun[0][1], begun[1][1]])))
    query_ends = [query_end(0, attended[0][0])]
    got, begun, out_sum, outputs, query_ends = hold((got, begun, out_sum, outputs, query_ends))
    line.absorb(got)
    in_shards = lambda values: values.reshape(devices, -1, values.shape[-1])
    back_way = [1] + bits[::-1]
    back_other = [1] + bits
    out_sum = in_shards(out_sum)
    out_steps = [
        ScatterWhole(out_sum[:, :out_half], back_way),
        ScatterWhole(out_sum[:, out_half:], back_other),
    ]

    sends, begun, out_sends, attended = hold(
        (line.sends(), begun, [job.send() for job in out_steps], attended)
    )
    got = line.move(sends)
    out_got = [job.move(value) for job, value in zip(out_steps, out_sends)]
    collected = [collect(attended[0][3])]
    attended.append(grads_attend(1, begun[1][2]))
    got, attended, out_got, begun = hold((got, attended, out_got, begun))
    line.absorb(got)
    for job, value in zip(out_steps, out_got):
        job.absorb(value)

    sends, attended, out_sends = hold(
        (line.sends(), attended, [job.send() for job in out_steps])
    )
    got = line.move(sends)
    collected.append(collect(attended[1][3]))
    out_got = [job.move(value) for job, value in zip(out_steps, out_sends)]
    latent_up_sum = low(
        jnp.concatenate([attended[0][1] + attended[1][1], attended[0][2] + attended[1][2]], axis=1)
    )
    query_sum = low(matmul_left(query_low, jnp.concatenate([attended[0][0], attended[1][0]])))
    query_ends.append(query_end(1, attended[1][0]))
    down_sum = low(matmul_left(first_low, jnp.concatenate([query_ends[0][0], query_ends[1][0]])))
    got, out_got, latent_up_sum, query_sum, down_sum, query_ends = hold(
        (got, out_got, latent_up_sum, query_sum, down_sum, query_ends)
    )
    line.absorb(got)
    for job, value in zip(out_steps, out_got):
        job.absorb(value)
    steps = [
        ScatterWhole(in_shards(query_sum), back_other),
        ScatterWhole(in_shards(latent_up_sum), back_way),
        ScatterWhole(in_shards(down_sum), back_way),
    ]

    small_steps = None
    while line.busy() or steps or small_steps != []:
        running = [job for job in out_steps + steps + (small_steps or []) if job.order]
        sends, values, query_ends, collected = hold(
            (line.sends(), [job.send() for job in running], query_ends, collected)
        )
        got = line.move(sends)
        values = [job.move(value) for job, value in zip(running, values)]
        if small_steps is None:
            ended = [
                grads_end(batch, query_ends[batch][0], collected[batch], begun[batch][0])
                for batch in range(batches)
            ]
            input_grads = [of[0] for of in ended]
            small_sum = matmul_left(first_low, jnp.concatenate([of[1] for of in ended]))
            places = lax.broadcasted_iota(jnp.int32, full_small.shape, 1) - gain_place
            gathered_gain = lambda gain: jnp.pad(
                gain.reshape(devices, -1), ((0, 0), (0, shard_rows - gain.shape[0] // devices))
            ).reshape(-1)
            gain_columns = [
                ended[0][2] + ended[1][2],
                begun[0][3] + begun[1][3],
                gathered_gain(query_ends[0][1] + query_ends[1][1]),
                gathered_gain(ended[0][3] + ended[1][3]),
            ]
            for place, gain in enumerate(gain_columns):
                small_sum = jnp.where(places == place, gain[:, None], small_sum)
            small_sum = low(small_sum)
            got, values, small_sum = hold((got, values, small_sum))
            small_steps = [ScatterWhole(in_shards(small_sum), back_other)]
        else:
            got, values = hold((got, values))
        line.absorb(got)
        for job, value in zip(running, values):
            job.absorb(value)
        if out_steps and not any(job.order for job in out_steps):
            line.add(jnp.concatenate([job.held[0] for job in out_steps]))
            out_steps = []
        if steps and not any(job.order for job in steps):
            line.add(*[job.held[0] for job in steps])
            steps = []
        if small_steps and not small_steps[0].order:
            line.add(small_steps[0].held[0])
            small_steps = []
    totals = [total.astype(jnp.float32) for total in line.held]
    ffn_totals = [jnp.concatenate(totals[2 * i : 2 * i + 2]) for i in (1, 2, 0)]
    out_total, query_total, latent_total, down_total, small_total = totals[6:]
    by_quad = query_total.reshape(-1, quads, QUAD * (DN + DR))
    query_up_total = jnp.concatenate(
        [
            by_quad[..., : QUAD * DN].reshape(-1, quads, QUAD, DN),
            by_quad[..., QUAD * DN :].reshape(-1, quads, QUAD, DR),
        ],
        axis=-1,
    ).reshape(query_up.shape)
    latent_up_total = jnp.concatenate(
        [
            latent_total[:, : H * DN].reshape(-1, H, DN),
            latent_total[:, H * DN :].reshape(-1, H, DV),
        ],
        axis=-1,
    ).reshape(latent_up.shape)
    return (
        jnp.stack(outputs)[None],
        jnp.stack(input_grads)[None],
        small_total[:, gain_place],
        down_total,
        small_total[: query_norm.shape[0], gain_place + 2],
        query_up_total,
        small_total[:, :gain_place],
        small_total[: latent_norm.shape[0], gain_place + 3],
        latent_up_total,
        out_total,
        small_total[:, gain_place + 1],
        ffn_totals[0],
        ffn_totals[1],
        ffn_totals[2],
    )


def solution(mesh):
    placed = (
        P("fsdp", None, "ctx", None),
        P("fsdp", None, "ctx", None),
        P("fsdp", None),
        P(),
        P("fsdp"),
        P("fsdp", None),
        P("fsdp"),
        P("fsdp", None),
        P("fsdp", None),
        P("fsdp"),
        P("fsdp", None),
        P("fsdp", None),
        P("fsdp"),
        P("fsdp", None),
        P("fsdp", None),
        P("fsdp", None),
    )
    return jax.shard_map(
        body,
        mesh=mesh,
        in_specs=placed,
        out_specs=(
            P("fsdp", None, "ctx", None),
            P("fsdp", None, "ctx", None),
            P("fsdp"),
            P("fsdp", None),
            P("fsdp"),
            P("fsdp", None),
            P("fsdp", None),
            P("fsdp"),
            P("fsdp", None),
            P("fsdp", None),
            P("fsdp"),
            P("fsdp", None),
            P("fsdp", None),
            P("fsdp", None),
        ),
        check_vma=False,
    )
```
